32 devices in a mesh: rep: 4 (over x, core), dom: 4 (over z), tp: 2 (over y).
Axes of the slice: x: 2, y: 2, z: 4, core: 2. Of those that a mesh axis runs over, the one named last changes fastest.
Arguments:
- features: bfloat16 [8, 1024, 256], P('rep', ('dom', 'tp')), may hold values from -6 to 6
- radial: bfloat16 [8, 32, 1024], P('rep', None, ('dom', 'tp')), may hold values from 0.019897461 to 0.125
- neighbours: int32 [8, 32, 1024], P('rep', None, ('dom', 'tp')), may hold values from -1 to 191, as said below
- halo_lists: int32 [8, 2, 256], P('rep', None, ('dom', 'tp')), may hold values from 0 to 127, as said below
- slab_counts: int32 [8, 8], P('rep', ('dom', 'tp')), may hold values from 64 to 128, as said below
- frame_labels: int32 [8], P('rep'), may hold values from 0 to 1, as said below
- w_a: bfloat16 [2, 256, 256], replicated, may hold values from -0.375 to 0.375
- w_c: bfloat16 [2, 256, 256], replicated, may hold values from -0.375 to 0.375
- w_b: bfloat16 [2, 256, 256], replicated, may hold values from -0.375 to 0.375
- readout: float32 [256], replicated, may hold values from -0.375 to 0.375
Outputs:
- grad_wa: float32 [2, 256, 256], replicated
- grad_wc: float32 [2, 256, 256], replicated
- grad_wb: float32 [2, 256, 256], replicated
- grad_readout: float32 [256], replicated
- bead_energy: float32 [8, 1024], P('rep', ('dom', 'tp'))
The draws below stay inside these ranges and needn't reach their ends.
Inputs may be any that keep to these rules, and one draw needn't show every extreme that they name: `neighbours`: an entry of a live bead names a live row of its own slab, or a halo row at 128 or above; empty slots are -1 and come after the filled ones; beads beyond the count have only empty slots. `halo_lists`: each entry names a live row of the sending slab. `slab_counts`: every frame has a full slab. `frame_labels`: exactly 4 frames carry each label.
All inputs are finite; a program needn't handle non-finite values.
Results may differ from the reference program's by a relative error of at most 0.008.
Values may be sent and summed in bfloat16 or wider, within the bound.
No kernel may reach another device: no remote copies, remote signals or barrier semaphores. Data moves between devices by JAX's collectives and lax.ppermute only.
A program may use at most 64 MiB of HBM per device.

```python
import math
import jax
import jax.numpy as jnp
from jax import lax

CHANNELS = 256
HIDDEN_SIZE = 256
DEGREE = 32
LAYERS = 2
SLAB_ROWS = 128
HALO_ROWS = 32
SLABS = 8
FRAMES = 8
BEADS = 1024
SEND_ROWS = 256


def counts_for(key):
    inner = jax.random.fold_in(key, 7)
    base_counts = jax.random.randint(inner, (FRAMES, SLABS), SLAB_ROWS // 2, SLAB_ROWS + 1)
    full_slab = jax.random.randint(jax.random.fold_in(inner, 1), (FRAMES, 1), 0, SLABS)
    return jnp.where(jnp.arange(SLABS)[None, :] == full_slab, SLAB_ROWS, base_counts).astype(jnp.int32)


def draw_slab_counts(key, part):
    return counts_for(key)


def draw_neighbours(key, part):
    counts = counts_for(key)
    key = jax.random.fold_in(key, 31)
    live_count = jnp.repeat(counts, SLAB_ROWS, axis=1)[:, None, :]
    row_index = jnp.arange(BEADS) % SLAB_ROWS
    degree = jax.random.randint(jax.random.fold_in(key, 1), (FRAMES, 1, BEADS), DEGREE // 2, DEGREE + 1)
    own_target = jax.random.randint(jax.random.fold_in(key, 2), (FRAMES, DEGREE, BEADS), 0, live_count)
    halo_target = jax.random.randint(jax.random.fold_in(key, 3), (FRAMES, DEGREE, BEADS), SLAB_ROWS, SLAB_ROWS + 2 * HALO_ROWS)
    use_halo = jax.random.randint(jax.random.fold_in(key, 4), (FRAMES, DEGREE, BEADS), 0, 4) == 0
    target = jnp.where(use_halo, halo_target, own_target)
    slot_index = jnp.arange(DEGREE)[None, :, None]
    keep_mask = (slot_index < degree) & (row_index[None, None, :] < live_count)
    return jnp.where(keep_mask, target, -1).astype(jnp.int32)


def draw_halo_lists(key, part):
    counts = counts_for(key)
    key = jax.random.fold_in(key, 41)
    live_count = jnp.repeat(counts, HALO_ROWS, axis=1)[:, None, :]
    drawn = jax.random.randint(key, (FRAMES, 2, SEND_ROWS), 0, live_count)
    entry_index = (jnp.arange(SEND_ROWS) % HALO_ROWS)[None, None, :]
    full_here = live_count == SLAB_ROWS
    drawn = jnp.where(full_here & (entry_index == 0), SLAB_ROWS - 1, drawn)
    drawn = jnp.where(full_here & (entry_index == 1), 0, drawn)
    return drawn.astype(jnp.int32)


def draw_frame_labels(key, part):
    key = jax.random.fold_in(key, 51)
    shuffled = jax.random.permutation(key, FRAMES)
    return (shuffled >= FRAMES // 2).astype(jnp.int32)


def block_levels(stream_key, dims, pieces, least, largest):
    factor_of, own = 1.0, jax.random.fold_in(stream_key, 6)
    for dim, blocks in pieces:
        draws = jnp.exp(jax.random.uniform(jax.random.fold_in(own, dim), (blocks,), jnp.float32, least / len(pieces), largest / len(pieces)))
        factor_of = factor_of * jnp.repeat(draws, dims[dim] // blocks).reshape([-1 if axis == dim else 1 for axis in range(len(dims))])
    return factor_of


def bell_draw(stream_key, shape, deviation, bound, split=(), kind=jnp.bfloat16):
    level = block_levels(stream_key, shape, split, -0.22, 0.18) if split else 1.0
    values = jax.random.normal(stream_key, shape, jnp.float32) * deviation * level
    return jnp.minimum(jnp.maximum(values, -bound), bound).astype(kind)


def setup_inputs(seed: int = 0) -> dict:
    seeds = jax.random.split(jax.random.key(seed), 11)
    features = bell_draw(seeds[0], (FRAMES, BEADS, CHANNELS), 1.0, 6.0, ((0, 4), (1, 8)))
    radial = jnp.clip(0.019897461 + 0.10510254 * jax.random.uniform(seeds[1], (FRAMES, DEGREE, BEADS), jnp.float32) ** block_levels(seeds[1], (FRAMES, DEGREE, BEADS), ((0, 4), (2, 8)), -0.2, 0.2), 0.019897461, 0.125).astype(jnp.bfloat16)
    neighbours = draw_neighbours(jax.random.fold_in(seeds[10], 71), 0)
    halo_lists = draw_halo_lists(jax.random.fold_in(seeds[10], 71), 0)
    slab_counts = draw_slab_counts(jax.random.fold_in(seeds[10], 71), 0)
    frame_labels = draw_frame_labels(jax.random.fold_in(seeds[10], 71), 0)
    w_a = bell_draw(seeds[6], (LAYERS, CHANNELS, HIDDEN_SIZE), CHANNELS ** -0.5, 0.375)
    w_c = bell_draw(seeds[7], (LAYERS, CHANNELS, HIDDEN_SIZE), CHANNELS ** -0.5, 0.375)
    w_b = bell_draw(seeds[8], (LAYERS, HIDDEN_SIZE, CHANNELS), HIDDEN_SIZE ** -0.5, 0.375)
    readout = bell_draw(seeds[9], (CHANNELS,), CHANNELS ** -0.5, 0.375, (), jnp.float32)
    return {"features": features, "radial": radial, "neighbours": neighbours, "halo_lists": halo_lists, "slab_counts": slab_counts, "frame_labels": frame_labels, "w_a": w_a, "w_c": w_c, "w_b": w_b, "readout": readout}


def slope_of(argument):
    sigmoid_value = jax.nn.sigmoid(argument)
    return sigmoid_value * (1.0 + argument * (1.0 - sigmoid_value))

def rows_of(lookup_table, indices):
    return jax.vmap(lambda block_rows, picked: block_rows[picked])(lookup_table, indices)

def add_rows(summed_rows, indices, addend):
    return jax.vmap(lambda block_rows, picked, extra: block_rows.at[picked].add(extra))(summed_rows, indices, addend)

def reference(features, radial, neighbours, halo_lists, slab_counts, frame_labels, w_a, w_c, w_b, readout):
    norm_scale = 1.0 / math.sqrt(BEADS)
    grads_a = [jnp.zeros((CHANNELS, HIDDEN_SIZE), jnp.float32) for layer_num in range(LAYERS)]
    grads_c = [jnp.zeros((CHANNELS, HIDDEN_SIZE), jnp.float32) for layer_num in range(LAYERS)]
    grads_b = [jnp.zeros((HIDDEN_SIZE, CHANNELS), jnp.float32) for layer_num in range(LAYERS)]
    grad_readout = jnp.zeros((CHANNELS,), jnp.float32)
    energies = []
    total_rows = SLAB_ROWS + 2 * HALO_ROWS
    for frame_num in range(FRAMES):
        state_now = features[frame_num].reshape(SLABS, SLAB_ROWS, CHANNELS)
        indices = neighbours[frame_num].reshape(DEGREE, SLABS, SLAB_ROWS).transpose(1, 0, 2)
        safe_index = jnp.maximum(indices, 0)
        edge_weight = radial[frame_num].reshape(DEGREE, SLABS, SLAB_ROWS).transpose(1, 0, 2).astype(jnp.float32)
        edge_weight = edge_weight * (indices >= 0).astype(jnp.float32)
        lists = halo_lists[frame_num].reshape(2, SLABS, HALO_ROWS)
        live_mask = (jnp.arange(SLAB_ROWS)[None, :] < slab_counts[frame_num][:, None]).astype(jnp.float32)
        frame_coef = jnp.where(frame_labels[frame_num] == 0, 2.0 / FRAMES, -2.0 / FRAMES).astype(jnp.float32) * norm_scale
        saved = []
        for layer_num in range(LAYERS):
            flat_rows = state_now.reshape(-1, CHANNELS)
            projected = jnp.dot(flat_rows, w_a[layer_num], preferred_element_type=jnp.float32).astype(jnp.bfloat16).reshape(SLABS, SLAB_ROWS, HIDDEN_SIZE)
            crossed = jnp.dot(flat_rows, w_c[layer_num], preferred_element_type=jnp.float32).reshape(SLABS, SLAB_ROWS, HIDDEN_SIZE)
            down_rows = rows_of(projected, lists[0])
            up_rows = rows_of(projected, lists[1])
            lookup_table = jnp.concatenate([projected, jnp.roll(up_rows, 1, axis=0), jnp.roll(down_rows, -1, axis=0)], axis=1)
            edge_sum = rows_of(lookup_table, safe_index).astype(jnp.float32) + crossed[:, None]
            gathered = lax.optimization_barrier(jnp.sum(jax.nn.silu(edge_sum) * edge_weight[..., None], axis=1)).astype(jnp.bfloat16)
            saved.append((state_now, lookup_table, crossed, gathered))
            update = jnp.dot(gathered.reshape(-1, HIDDEN_SIZE), w_b[layer_num], preferred_element_type=jnp.float32).reshape(SLABS, SLAB_ROWS, CHANNELS)
            state_now = (state_now.astype(jnp.float32) + update).astype(jnp.bfloat16)
        final_state = state_now.astype(jnp.float32)
        activated = jax.nn.silu(final_state)
        energies.append((live_mask * lax.optimization_barrier(jnp.sum(activated * readout, axis=-1))).reshape(-1))
        grad_readout = grad_readout + frame_coef * lax.optimization_barrier(jnp.sum(live_mask[..., None] * activated, axis=(0, 1)))
        cotangent = (frame_coef * live_mask)[..., None] * readout * slope_of(final_state)
        for layer_num in reversed(range(LAYERS)):
            state_in, lookup_table, crossed, gathered = saved[layer_num]
            cot_low = cotangent.astype(jnp.bfloat16).reshape(-1, CHANNELS)
            grads_b[layer_num] = grads_b[layer_num] + jnp.dot(gathered.reshape(-1, HIDDEN_SIZE).T, cot_low, preferred_element_type=jnp.float32)
            cot_gathered = jnp.dot(cot_low, w_b[layer_num].T, preferred_element_type=jnp.float32).reshape(SLABS, SLAB_ROWS, HIDDEN_SIZE)
            edge_sum = rows_of(lookup_table, safe_index).astype(jnp.float32) + crossed[:, None]
            cot_edge = cot_gathered[:, None] * edge_weight[..., None] * slope_of(edge_sum)
            cot_cross = lax.optimization_barrier(jnp.sum(cot_edge, axis=1))
            cot_table = add_rows(jnp.zeros((SLABS, total_rows, HIDDEN_SIZE), jnp.float32), safe_index, cot_edge)
            cot_pre = add_rows(cot_table[:, :SLAB_ROWS], lists[1], jnp.roll(cot_table[:, SLAB_ROWS:SLAB_ROWS + HALO_ROWS], -1, axis=0))
            cot_pre = add_rows(cot_pre, lists[0], jnp.roll(cot_table[:, SLAB_ROWS + HALO_ROWS:], 1, axis=0))
            pre_low = cot_pre.astype(jnp.bfloat16).reshape(-1, HIDDEN_SIZE)
            cross_low = cot_cross.astype(jnp.bfloat16).reshape(-1, HIDDEN_SIZE)
            flat_rows = state_in.reshape(-1, CHANNELS)
            grads_a[layer_num] = grads_a[layer_num] + jnp.dot(flat_rows.T, pre_low, preferred_element_type=jnp.float32)
            grads_c[layer_num] = grads_c[layer_num] + jnp.dot(flat_rows.T, cross_low, preferred_element_type=jnp.float32)
            if layer_num > 0:
                partial_value = jnp.dot(pre_low, w_a[layer_num].T, preferred_element_type=jnp.float32)
                partial_value = partial_value + jnp.dot(cross_low, w_c[layer_num].T, preferred_element_type=jnp.float32)
                cotangent = cotangent + partial_value.reshape(SLABS, SLAB_ROWS, CHANNELS)
    return (jnp.stack(grads_a), jnp.stack(grads_c), jnp.stack(grads_b), grad_readout, jnp.stack(energies))
```

```python
import functools
import math

import jax
import jax.numpy as jnp
from jax import lax
from jax.experimental import pallas as pl
from jax.experimental.pallas import tpu as pltpu
from jax.sharding import PartitionSpec as P

BF16, F32 = jnp.bfloat16, jnp.float32
MEBI = 1024 * 1024
SUB = 16
RING = ("dom", "tp")
EVERY = ("rep", "dom", "tp")


def mul(a, b):
    return jnp.dot(a, b, preferred_element_type=F32)


def mul_nt(a, b):
    return lax.dot_general(a, b, (((1,), (1,)), ((), ())), preferred_element_type=F32)


def mul_tn(a, b):
    return lax.dot_general(a, b, (((0,), (0,)), ((), ())), preferred_element_type=F32)


def packed_halves(both):
    rows, lanes = both.shape[0] // 2, both.shape[1] // 2
    low, high = both[:rows], both[rows:]
    first = jnp.concatenate([low[:, :lanes], high[:, :lanes]], axis=1)
    second = jnp.concatenate([low[:, lanes:], high[:, lanes:]], axis=1)
    return first, second


def unpacked_halves(first, second):
    lanes = first.shape[1] // 2
    low = jnp.concatenate([first[:, :lanes], second[:, :lanes]], axis=1)
    high = jnp.concatenate([first[:, lanes:], second[:, lanes:]], axis=1)
    return jnp.concatenate([low, high], axis=0)


def send_lanes(even, list_ref, beads):
    parts = []
    for side in range(2):
        for frame in range(list_ref.shape[0]):
            down, up = list_ref[frame, 0:1, :], list_ref[frame, 1:2, :]
            parts.append((jnp.where(even, down, up) if side else jnp.where(even, up, down)) + frame * beads)
    return jnp.concatenate(parts, axis=1)


def write_halo(first_ref, second_ref, both):
    first, second = packed_halves(both)
    first_ref[...] = first.astype(BF16)
    second_ref[...] = second.astype(BF16)


def read_halo(first_ref, second_ref):
    return unpacked_halves(first_ref[...].astype(F32), second_ref[...].astype(F32)).astype(BF16)


def copies_of(pairs, sems):
    copies = [pltpu.make_async_copy(source, target, sems.at[n]) for n, (source, target) in enumerate(pairs)]
    for copy in copies:
        copy.start()
    return copies


def select_kernel(
    where_ref, feat_hbm, list_hbm, state_ref, select_ref, first_ref, second_ref, feat_ref, list_ref, sems
):
    list_copy, feat_copy = copies_of([(list_hbm, list_ref), (feat_hbm, feat_ref)], sems)
    list_copy.wait()
    frames, beads, channels = feat_ref.shape
    lanes = frames * beads
    sent = send_lanes(where_ref[1] == 0, list_ref, beads)
    row = lax.broadcasted_iota(jnp.int32, (lanes, sent.shape[1]), 0)
    select = jnp.where(row == sent, 1.0, 0.0).astype(BF16)
    feat_copy.wait()
    state = feat_ref[...].reshape(lanes, channels).astype(F32).T.astype(BF16)
    write_halo(first_ref, second_ref, mul(state, select))
    state_ref[...] = state
    select_ref[...] = select


def write_onehot(onehot_ref, slots_ref):
    frames, degree, beads = slots_ref.shape
    row = lax.broadcasted_iota(jnp.int32, (onehot_ref.shape[1], beads), 0)
    for frame in range(frames):
        for slot in range(degree):
            hit = row == slots_ref[frame, slot : slot + 1, :]
            onehot_ref[frame, :, slot * beads : (slot + 1) * beads] = jnp.where(hit, 1.0, 0.0).astype(BF16)


def prepare_kernel(
    halo, where_ref, count_ref, label_ref, neigh_hbm, radial_hbm, wa_hbm, wc_hbm, wb_hbm, readout_hbm, state_ref,
    onehot_ref, edge_ref, wa_ref, wc_ref, wb_ref, wta_ref, wtc_ref, wtb_ref, own_ref, cross_ref, live_ref, sign_ref, wide_ref,
    neigh_ref, radial_ref, readout_ref, slots_ref, sems,
):
    frames, degree, beads = neigh_ref.shape
    pairs = [(neigh_hbm, neigh_ref), (radial_hbm, radial_ref), (wa_hbm, wa_ref), (wc_hbm, wc_ref), (wb_hbm, wb_ref)]
    pairs.append((readout_hbm, readout_ref))
    copies = copies_of(pairs, sems)
    copies[0].wait()
    copies[1].wait()
    odd = where_ref[1] != 0
    bead = lax.broadcasted_iota(jnp.int32, (1, beads), 1)
    for frame in range(frames):
        live = jnp.where(bead < count_ref[frame, 0], 1.0, 0.0)
        lanes = slice(frame * beads, (frame + 1) * beads)
        live_ref[:, lanes] = live
        sign_ref[:, lanes] = jnp.where(label_ref[frame] == 0, live, -live)
        neigh = neigh_ref[frame]
        weight = jnp.where(neigh >= 0, radial_ref[frame].astype(F32), 0.0)
        entry = neigh - beads
        upper = entry >= halo
        entry = jnp.where(upper, entry - halo, entry) + (beads + frame * halo)
        upper = jnp.where(upper, 1, 0)
        side = jnp.where(odd, upper, 1 - upper)
        slots_ref[frame] = jnp.where(neigh < beads, neigh, entry + side * (frames * halo))
        for slot in range(degree):
            edge_ref[frame, slot] = jnp.broadcast_to(weight[slot : slot + 1, :], (SUB, beads)).astype(BF16)
    write_onehot(onehot_ref, slots_ref)
    for copy in copies[2:]:
        copy.wait()
    for layer in range(wa_ref.shape[0]):
        wta_ref[layer] = wa_ref[layer].astype(F32).T.astype(BF16)
        wtc_ref[layer] = wc_ref[layer].astype(F32).T.astype(BF16)
        wtb_ref[layer] = wb_ref[layer].astype(F32).T.astype(BF16)
    own_ref[...] = mul(wta_ref[0], state_ref[...]).astype(BF16)
    cross_ref[...] = mul(wtc_ref[0], state_ref[...])
    wide = readout_ref[...].reshape(1, -1)
    wide_ref[...] = jnp.broadcast_to(wide, (wide_ref.shape[1], wide.shape[1])).T


def edges(onehot_ref, edge_ref, own, halo, cross, slope_ref, total_ref, slope_total_ref, group=4):
    frames, degree, _, beads = edge_ref.shape
    hidden = own.shape[0]
    blocks = hidden // SUB
    for frame in range(frames):
        lanes = slice(frame * beads, (frame + 1) * beads)
        table = jnp.concatenate([own[:, lanes], halo], axis=1) * jnp.asarray(0.5, BF16)
        half_cross = cross[:, lanes] * 0.5
        wide_cross = jnp.concatenate([half_cross] * group, axis=1)
        total_ref[:, lanes] = jnp.zeros((hidden, beads), F32)
        slope_total_ref[:, lanes] = jnp.zeros((hidden, beads), F32)

        def step(index, carry):
            at = slice(index * group * beads, (index + 1) * group * beads)
            half = (mul(table, onehot_ref[frame, :, at]) + wide_cross).astype(BF16)
            turn = jnp.tanh(half)
            act = half + half * turn
            slope = (1 + turn) + half * (1 - turn * turn)
            act_sum, slope_sum = None, None
            kept = []
            for part in range(group):
                here = slice(part * beads, (part + 1) * beads)
                weight = edge_ref[frame, index * group + part]
                a = (act[:, here].reshape(blocks, SUB, beads) * weight[None]).reshape(hidden, beads)
                s = (slope[:, here].reshape(blocks, SUB, beads) * (weight * jnp.asarray(0.5, BF16))[None]).reshape(hidden, beads)
                kept.append(s)
                act_sum = a if act_sum is None else act_sum + a
                slope_sum = s if slope_sum is None else slope_sum + s
            slope_ref[frame, :, at] = jnp.concatenate(kept, axis=1)
            total_ref[:, lanes] += act_sum.astype(F32)
            slope_total_ref[:, lanes] += slope_sum.astype(F32)
            return carry

        for index in range(degree // group):
            step(index, 0)


def scatter(onehot_ref, slope_ref, cot_gathered, frame, beads, group=8):
    count = slope_ref.shape[2] // beads
    lanes = slice(frame * beads, (frame + 1) * beads)
    wide = jnp.concatenate([cot_gathered[:, lanes]] * group, axis=1)
    total = None
    for index in range(count // group):
        at = slice(index * group * beads, (index + 1) * group * beads)
        part = mul_nt(slope_ref[frame, :, at] * wide, onehot_ref[frame, :, at])
        total = part if total is None else total + part
    return total


def first_kernel(
    hf_ref, hs_ref, onehot_ref, edge_ref, wta_ref, wtb_ref, own_ref, cross_ref, state_ref, select_ref,
    next_ref, first_ref, second_ref, halo_ref, gathered_ref, slope_ref, slope_total_ref,
    total_ref,
):
    halo = read_halo(hf_ref, hs_ref)
    halo_ref[...] = halo
    halo_rows = mul(wta_ref[0], halo).astype(BF16)
    edges(onehot_ref, edge_ref, own_ref[...], halo_rows, cross_ref[...], slope_ref, total_ref, slope_total_ref)
    gathered = total_ref[...].astype(BF16)
    gathered_ref[...] = gathered
    state = (state_ref[...].astype(F32) + mul(wtb_ref[0], gathered)).astype(BF16)
    next_ref[...] = state
    write_halo(first_ref, second_ref, mul(state, select_ref[...]))


def middle_kernel(
    scale,
    hf_ref, hs_ref, onehot_ref, edge_ref, wta_ref, wtc_ref, wtb_ref, wb_ref, state_ref, live_ref, sign_ref, readout_ref,
    energy_ref, grad_readout_ref, cot_ref, first_ref, second_ref, cot_own_ref, cot_halo_ref, cot_cross_ref,
    halo_ref, gathered_ref, cot_low_ref,
    slope_ref, slope_total_ref, total_ref,
):
    last = wta_ref.shape[0] - 1
    beads = edge_ref.shape[3]
    frames = edge_ref.shape[0]
    halo = read_halo(hf_ref, hs_ref)
    halo_ref[...] = halo
    state = state_ref[...]
    own = mul(wta_ref[last], state).astype(BF16)
    cross = mul(wtc_ref[last], state)
    halo_rows = mul(wta_ref[last], halo).astype(BF16)
    edges(onehot_ref, edge_ref, own, halo_rows, cross, slope_ref, total_ref, slope_total_ref)
    gathered = total_ref[...].astype(BF16)
    gathered_ref[...] = gathered
    final = (state.astype(F32) + mul(wtb_ref[last], gathered)).astype(BF16).astype(F32)
    sigmoid = jax.nn.sigmoid(final)
    activated = final * sigmoid
    readout = jnp.concatenate([readout_ref[...]] * frames, axis=1)
    live = live_ref[...]
    sign = sign_ref[...]
    energy = live * jnp.sum(activated * readout, axis=0, keepdims=True)
    for frame in range(frames):
        energy_ref[frame : frame + 1, :] = energy[:, frame * beads : (frame + 1) * beads]
    signs = jnp.broadcast_to(sign, (SUB, sign.shape[1])).astype(BF16)
    grad_readout_ref[...] = mul_nt(signs, activated.astype(BF16)) * scale
    cot = (sign * scale) * readout * (sigmoid * (1.0 + final * (1.0 - sigmoid)))
    cot_ref[...] = cot
    cot_low = cot.astype(BF16)
    cot_low_ref[...] = cot_low
    cot_gathered = mul(wb_ref[last], cot_low)
    cot_cross_ref[...] = (cot_gathered * slope_total_ref[...]).astype(BF16)
    cot_gathered = cot_gathered.astype(BF16)
    cot_halo = None
    for frame in range(frames):
        part = scatter(onehot_ref, slope_ref, cot_gathered, frame, beads)
        cot_own_ref[:, frame * beads : (frame + 1) * beads] = part[:, :beads]
        cot_halo = part[:, beads:] if cot_halo is None else cot_halo + part[:, beads:]
    write_halo(first_ref, second_ref, cot_halo)
    cot_halo_ref[...] = cot_halo.astype(BF16)


def put_slots(slots_ref, me, grads, base=0):
    slots = slots_ref.shape[0]
    rows = grads[0].shape[0] // slots
    for chunk in range(slots):
        slot = jnp.bitwise_xor(me, chunk)
        for number, grad in enumerate(grads):
            slots_ref[slot, base + number * rows : base + (number + 1) * rows, :] = grad[chunk * rows : (chunk + 1) * rows]


def upper_grads_kernel(
    me_ref, state_ref, halo_ref, gathered_ref, cot_low_ref, cot_own_ref, cot_halo_ref, cot_cross_ref, grad_readout_ref, slots_ref
):
    me = me_ref[0]
    state = state_ref[...]
    grad_a = mul_nt(state, cot_own_ref[...].astype(BF16)) + mul_nt(halo_ref[...], cot_halo_ref[...])
    grad_c = mul_nt(state, cot_cross_ref[...])
    grad_b = mul_nt(gathered_ref[...], cot_low_ref[...])
    put_slots(slots_ref, me, [grad_a, grad_c, grad_b], SUB)
    row = lax.broadcasted_iota(jnp.int32, (SUB, slots_ref.shape[2]), 0)
    only = jnp.where(row == 0, grad_readout_ref[...], 0.0)
    for slot in range(slots_ref.shape[0]):
        slots_ref[slot, :SUB, :] = only


def lower_kernel(
    me_ref, bf_ref, bs_ref, select_ref, cot_own_ref, cot_cross_ref, cot_ref, wa_ref, wc_ref, wb_ref,
    onehot_ref, slope_ref, slope_total_ref, state_ref, halo_ref, gathered_ref,
    slots_ref,
):
    me = me_ref[0]
    frames = onehot_ref.shape[0]
    beads = cot_ref.shape[1] // frames
    back = read_halo(bf_ref, bs_ref)
    cot_own = (cot_own_ref[...] + mul_nt(back, select_ref[...])).astype(BF16)
    cot = cot_ref[...] + mul(wa_ref[1], cot_own) + mul(wc_ref[1], cot_cross_ref[...])
    cot_low = cot.astype(BF16)
    state = state_ref[...]
    grad_b = mul_nt(gathered_ref[...], cot_low)
    cot_gathered = mul(wb_ref[0], cot_low)
    grad_c = mul_nt(state, (cot_gathered * slope_total_ref[...]).astype(BF16))
    cot_gathered = cot_gathered.astype(BF16)
    cot_halo, grad_a = None, None
    for frame in range(frames):
        lanes = slice(frame * beads, (frame + 1) * beads)
        part = scatter(onehot_ref, slope_ref, cot_gathered, frame, beads)
        here = mul_nt(state[:, lanes], part[:, :beads].astype(BF16))
        grad_a = here if grad_a is None else grad_a + here
        cot_halo = part[:, beads:] if cot_halo is None else cot_halo + part[:, beads:]
    grad_a = grad_a + mul_nt(halo_ref[...], cot_halo.astype(BF16))
    put_slots(slots_ref, me, [grad_a, grad_c, grad_b])


def finish_kernel(me_ref, *refs):
    near, far = refs[:4], refs[4]
    wa_ref, wc_ref, wb_ref, readout_ref = refs[5:]
    me = me_ref[0]
    rows = (far.shape[1] - SUB) // 6
    for slot in range(8):
        source = near[slot] if slot < 4 else far.at[slot - 4]
        chunk = jnp.bitwise_xor(me, slot)
        place = pl.ds(pl.multiple_of(chunk * rows, rows), rows)
        for layer, base in ((1, SUB), (0, SUB + 3 * rows)):
            for number, ref in enumerate((wa_ref, wc_ref, wb_ref)):
                ref[layer, place, :] = source[base + number * rows : base + (number + 1) * rows, :].astype(F32)
        if slot == 0:
            head = source[:SUB, :].astype(F32)
            readout_ref[...] = head[0] + head[1]


def kernel_call(body, outs, args, scratch=(), flops=0, smem=0, far=0, limit=24):
    spaces = [pltpu.SMEM] * smem + [pltpu.HBM] * far + [pltpu.VMEM] * (len(args) - smem - far)
    args = [pltpu.with_memory_space_constraint(a, pltpu.HBM) if s is pltpu.HBM else a for a, s in zip(args, spaces)]
    return pl.pallas_call(
        body,
        out_shape=outs,
        in_specs=[pl.BlockSpec(memory_space=space) for space in spaces],
        out_specs=jax.tree.map(
            lambda out: pl.BlockSpec(memory_space=pltpu.HBM if getattr(out, "memory_space", None) is pltpu.HBM else pltpu.VMEM), outs
        ),
        scratch_shapes=list(scratch),
        compiler_params=pltpu.CompilerParams(vmem_limit_bytes=limit * MEBI),
        cost_estimate=pl.CostEstimate(flops=flops, bytes_accessed=0, transcendentals=0),
    )(*args)


def near(shape, dtype=BF16):
    return pltpu.VMEM(shape, dtype)


def swapped(value, kind):
    count = lax.axis_size(RING)
    if kind == 0:
        pairs = [(s, s ^ 1) for s in range(count)]
    else:
        pairs = [(s, (s + 1) % count if s % 2 else (s - 1) % count) for s in range(count)]
    return lax.ppermute(value, RING, pairs)


def partner(value, axis, bits):
    return lax.ppermute(value, axis, [(s, s ^ bits) for s in range(lax.axis_size(axis))])


def summed(*terms):
    total = terms[0].astype(F32)
    for term in terms[1:]:
        total = total + term.astype(F32)
    whole = total[..., 0:1, :] + total[..., 1:2, :]
    upper = lax.reduce_precision(whole, 8, 7)
    row = lax.broadcasted_iota(jnp.int32, total.shape, total.ndim - 2)
    return jnp.where(row == 0, upper, jnp.where(row == 1, whole - upper, total)).astype(BF16)


def plane(value, x, y):
    rep, dom, tp = (lax.axis_size(a) for a in EVERY)
    flip = (2 * dom * tp if x else 0) + (1 if y else 0)
    return lax.ppermute(value, EVERY, [(s, s ^ flip) for s in range(rep * dom * tp)])


def along_dom(mine):
    count, bit = lax.axis_size("dom"), 1
    while bit < count:
        flips = [bit] if 2 * bit >= count else [bit, 2 * bit, 3 * bit]
        mine = summed(mine, *[partner(mine, "dom", flip) for flip in flips])
        bit *= 4
    return mine


def reduce_slots(slots):
    part = slots[:4] + partner(slots[4:], "rep", 1)
    mine = summed(part[0], plane(part[1], 0, 1), plane(part[2], 1, 0), plane(part[3], 1, 1))
    mine = along_dom(mine)
    close = [mine, plane(mine, 0, 1), plane(mine, 1, 0), plane(mine, 1, 1)]
    return close, partner(jnp.stack(close), "rep", 1)


def local(features, radial, neighbours, halo_lists, slab_counts, frame_labels, w_a, w_c, w_b, readout):
    frames, beads, channels = features.shape
    hidden, layers = w_a.shape[2], w_a.shape[0]
    degree, halo = radial.shape[1], halo_lists.shape[2]
    lanes, halo_lanes = frames * beads, 2 * frames * halo
    rows = beads + halo_lanes
    scale = (2.0 / (frames * lax.axis_size("rep"))) / math.sqrt(beads * lax.axis_size(RING))
    rep = lax.axis_index("rep")
    me = (lax.rem(rep, 2) * 4 + (rep // 2) * 2 + lax.axis_index("tp")).astype(jnp.int32)
    where = jnp.stack([me, lax.rem(lax.axis_index(RING), 2).astype(jnp.int32)])

    half = (channels // 2, halo_lanes)
    state, select, first, second = kernel_call(
        select_kernel,
        (near((channels, lanes)), near((lanes, halo_lanes)), near(half), near(half)),
        (where, features, halo_lists),
        scratch=[
            pltpu.VMEM(features.shape, BF16),
            pltpu.VMEM(halo_lists.shape, jnp.int32),
            pltpu.SemaphoreType.DMA((2,)),
        ],
        smem=1,
        far=2,
    )
    second, first = swapped(second, 1), swapped(first, 0)
    weights = [near((layers, channels, hidden)), near((layers, channels, hidden)), near((layers, hidden, channels))]
    turned = [near((layers, hidden, channels)), near((layers, hidden, channels)), near((layers, channels, hidden))]
    onehot_type = near((frames, rows, degree * beads))
    onehot, edge, wa, wc, wb, wta, wtc, wtb, own, cross, live, sign, wide = kernel_call(
        functools.partial(prepare_kernel, halo),
        (
            onehot_type,
            near((frames, degree, SUB, beads)),
            *weights,
            *turned,
            near((hidden, lanes)),
            near((hidden, lanes), F32),
            near((1, lanes), F32),
            near((1, lanes), F32),
            near((channels, beads), F32),
        ),
        (where, slab_counts, frame_labels, neighbours, radial, w_a, w_c, w_b, readout, state),
        scratch=[
            pltpu.VMEM(neighbours.shape, jnp.int32),
            pltpu.VMEM(radial.shape, BF16),
            pltpu.VMEM(readout.shape, F32),
            pltpu.VMEM(neighbours.shape, jnp.int32),
            pltpu.SemaphoreType.DMA((6,)),
        ],
        smem=3,
        far=6,
        flops=2 * 10**9,
    )
    totals = (hidden, lanes)
    edge_slopes = (frames, hidden, degree * beads)
    state1, first, second, halo0, gathered0, slope0, slope_total0 = kernel_call(
        first_kernel,
        (
            near((channels, lanes)),
            near(half),
            near(half),
            near((channels, halo_lanes)),
            near(totals),
            near(edge_slopes),
            near(totals, F32),
        ),
        (first, second, onehot, edge, wta, wtb, own, cross, state, select),
        scratch=[pltpu.VMEM(totals, F32)],
        flops=4 * 10**9,
    )
    second, first = swapped(second, 1), swapped(first, 0)
    energy, grad_readout, cot, first, second, cot_own, cot_halo, cot_cross, halo1, gathered1, cot_low1 = kernel_call(
        functools.partial(middle_kernel, scale),
        (
            jax.ShapeDtypeStruct((frames, beads), F32),
            near((SUB, channels), F32),
            near((channels, lanes), F32),
            near(half),
            near(half),
            near(totals, F32),
            near((hidden, halo_lanes)),
            near(totals),
            near((channels, halo_lanes)),
            near(totals),
            near((channels, lanes)),
        ),
        (first, second, onehot, edge, wta, wtc, wtb, wb, state1, live, sign, wide),
        scratch=[pltpu.VMEM(edge_slopes, BF16), pltpu.VMEM(totals, F32), pltpu.VMEM(totals, F32)],
        flops=6 * 10**9,
    )
    second, first = swapped(second, 1), swapped(first, 0)
    chunk = hidden // 8
    upper_slots = kernel_call(
        upper_grads_kernel,
        near((8, SUB + 3 * chunk, channels), F32),
        (where, state1, halo1, gathered1, cot_low1, cot_own, cot_halo, cot_cross, grad_readout),
        smem=1,
        flops=10**9,
    )
    lower_slots = kernel_call(
        lower_kernel,
        near((8, 3 * chunk, channels), F32),
        (
            where, first, second, select, cot_own, cot_cross, cot, wa, wc, wb,
            onehot, slope0, slope_total0, state, halo0, gathered0,
        ),
        smem=1,
        flops=4 * 10**9,
    )
    close, far = reduce_slots(jnp.concatenate([upper_slots, lower_slots], axis=1))
    grad = jax.ShapeDtypeStruct((layers, channels, hidden), F32)
    grad_wa, grad_wc, grad_wb, grad_readout = kernel_call(
        finish_kernel,
        (grad, grad, grad, jax.ShapeDtypeStruct((channels,), F32)),
        (where, *close, far),
        smem=1,
    )
    return grad_wa, grad_wc, grad_wb, grad_readout, energy


def solution(mesh):
    placed = (
        P("rep", RING, None),
        P("rep", None, RING),
        P("rep", None, RING),
        P("rep", None, RING),
        P("rep", RING),
        P("rep"),
        P(),
        P(),
        P(),
        P(),
    )
    return jax.shard_map(
        local,
        mesh=mesh,
        in_specs=placed,
        out_specs=(P(), P(), P(), P(), P("rep", RING)),
        check_vma=False,
    )
```

```python
import functools
import math

import jax
import jax.numpy as jnp
from jax import lax
from jax.experimental import pallas as pl
from jax.experimental.pallas import tpu as pltpu
from jax.sharding import PartitionSpec as P

BF16, F16, F32 = jnp.bfloat16, jnp.float16, jnp.float32
MEBI = 1024 * 1024
SUB = 16
RING = ("dom", "tp")
EVERY = ("rep", "dom", "tp")


def mul(a, b):
    return jnp.dot(a, b, preferred_element_type=F32)


def mul_nt(a, b):
    return lax.dot_general(a, b, (((1,), (1,)), ((), ())), preferred_element_type=F32)


def mul_tn(a, b):
    return lax.dot_general(a, b, (((0,), (0,)), ((), ())), preferred_element_type=F32)


def packed_halves(both):
    rows, lanes = both.shape[0] // 2, both.shape[1] // 2
    low, high = both[:rows], both[rows:]
    first = jnp.concatenate([low[:, :lanes], high[:, :lanes]], axis=1)
    second = jnp.concatenate([low[:, lanes:], high[:, lanes:]], axis=1)
    return first, second


def unpacked_halves(first, second):
    lanes = first.shape[1] // 2
    low = jnp.concatenate([first[:, :lanes], second[:, :lanes]], axis=1)
    high = jnp.concatenate([first[:, lanes:], second[:, lanes:]], axis=1)
    return jnp.concatenate([low, high], axis=0)


def send_lanes(even, list_ref, beads):
    parts = []
    for side in range(2):
        for frame in range(list_ref.shape[0]):
            down, up = list_ref[frame, 0:1, :], list_ref[frame, 1:2, :]
            parts.append((jnp.where(even, down, up) if side else jnp.where(even, up, down)) + frame * beads)
    return jnp.concatenate(parts, axis=1)


def write_halo(first_ref, second_ref, both):
    first, second = packed_halves(both)
    first_ref[...] = first.astype(BF16)
    second_ref[...] = second.astype(BF16)


def read_halo(first_ref, second_ref):
    return unpacked_halves(first_ref[...].astype(F32), second_ref[...].astype(F32)).astype(BF16)


def copies_of(pairs, sems):
    copies = [pltpu.make_async_copy(source, target, sems.at[n]) for n, (source, target) in enumerate(pairs)]
    for copy in copies:
        copy.start()
    return copies


def select_kernel(
    where_ref, feat_hbm, list_hbm, neigh_hbm, radial_hbm,
    state_ref, select_ref, first_ref, second_ref, neigh_ref, radial_ref,
    feat_ref, list_ref, sems,
):
    pairs = [(list_hbm, list_ref), (feat_hbm, feat_ref), (neigh_hbm, neigh_ref), (radial_hbm, radial_ref)]
    list_copy, feat_copy, *others = copies_of(pairs, sems)
    list_copy.wait()
    frames, beads, channels = feat_ref.shape
    lanes = frames * beads
    sent = send_lanes(where_ref[1] == 0, list_ref, beads)
    row = lax.broadcasted_iota(jnp.int32, (lanes, sent.shape[1]), 0)
    select = jnp.where(row == sent, 1.0, 0.0).astype(BF16)
    feat_copy.wait()
    state = feat_ref[...].reshape(lanes, channels).astype(F32).T.astype(BF16)
    write_halo(first_ref, second_ref, mul(state, select))
    state_ref[...] = state
    select_ref[...] = select
    for copy in others:
        copy.wait()


def write_onehot(onehot_ref, slots_ref):
    frames, degree, beads = slots_ref.shape
    row = lax.broadcasted_iota(jnp.int32, (onehot_ref.shape[1], beads), 0)
    for frame in range(frames):
        for slot in range(degree):
            hit = row == slots_ref[frame, slot : slot + 1, :]
            onehot_ref[frame, :, slot * beads : (slot + 1) * beads] = jnp.where(hit, 1.0, 0.0).astype(BF16)


def prepare_kernel(
    halo, where_ref, wa_hbm, wc_hbm, wb_hbm, readout_hbm, state_ref, neigh_ref, radial_ref,
    onehot_ref, edge_ref, wa_ref, wc_ref, wb_ref, readout_ref, wta_ref, wtb_ref, own_ref, cross_ref,
    slots_ref, sems,
):
    frames, degree, beads = neigh_ref.shape
    pairs = [(wa_hbm, wa_ref), (wc_hbm, wc_ref), (wb_hbm, wb_ref), (readout_hbm, readout_ref)]
    copies = copies_of(pairs, sems)
    odd = where_ref[1] != 0
    for frame in range(frames):
        neigh = neigh_ref[frame]
        weight = jnp.where(neigh >= 0, radial_ref[frame].astype(F32), 0.0)
        entry = neigh - beads
        upper = entry >= halo
        entry = jnp.where(upper, entry - halo, entry) + (beads + frame * halo)
        upper = jnp.where(upper, 1, 0)
        side = jnp.where(odd, upper, 1 - upper)
        slots_ref[frame] = jnp.where(neigh < beads, neigh, entry + side * (frames * halo))
        for slot in range(degree):
            edge_ref[frame, slot] = jnp.broadcast_to(weight[slot : slot + 1, :], (SUB, beads)).astype(BF16)
    write_onehot(onehot_ref, slots_ref)
    for copy in copies:
        copy.wait()
    turned = wa_ref[0].astype(F32).T.astype(BF16)
    wta_ref[...] = turned
    wtb_ref[...] = wb_ref[0].astype(F32).T.astype(BF16)
    own_ref[...] = mul(turned, state_ref[...]).astype(BF16)
    cross_ref[...] = mul(wc_ref[0].astype(F32).T.astype(BF16), state_ref[...])


def later_kernel(
    frame_ref, _after, wa_ref, wc_ref, wb_ref, readout_ref, wta_ref, wtc_ref, wtb_ref, wide_ref, live_ref, sign_ref
):
    for source, target in ((wa_ref, wta_ref), (wc_ref, wtc_ref), (wb_ref, wtb_ref)):
        target[...] = source[source.shape[0] - 1].astype(F32).T.astype(BF16)
    wide = readout_ref[...].reshape(1, -1)
    beads = wide_ref.shape[1]
    wide_ref[...] = jnp.broadcast_to(wide, (beads, wide.shape[1])).T
    frames = live_ref.shape[1] // beads
    bead = lax.broadcasted_iota(jnp.int32, (1, beads), 1)
    for frame in range(frames):
        live = jnp.where(bead < frame_ref[frame], 1.0, 0.0)
        here = slice(frame * beads, (frame + 1) * beads)
        live_ref[:, here] = live
        sign_ref[:, here] = jnp.where(frame_ref[frames + frame] == 0, live, -live)


def edges(onehot_ref, edge_ref, own, halo, cross, slope_ref, total_ref, slope_total_ref, group=4):
    frames, degree, _, beads = edge_ref.shape
    hidden = own.shape[0]
    blocks = hidden // SUB
    for frame in range(frames):
        lanes = slice(frame * beads, (frame + 1) * beads)
        table = jnp.concatenate([own[:, lanes], halo], axis=1) * jnp.asarray(0.5, BF16)
        half_cross = cross[:, lanes] * 0.5
        wide_cross = jnp.concatenate([half_cross] * group, axis=1)
        total_ref[:, lanes] = jnp.zeros((hidden, beads), F32)
        slope_total_ref[:, lanes] = jnp.zeros((hidden, beads), F32)

        def step(index, carry):
            at = slice(index * group * beads, (index + 1) * group * beads)
            half = (mul(table, onehot_ref[frame, :, at]) + wide_cross).astype(BF16)
            turn = jnp.tanh(half)
            act = half + half * turn
            slope = (1 + turn) + half * (1 - turn * turn)
            act_sum, slope_sum = None, None
            kept = []
            for part in range(group):
                here = slice(part * beads, (part + 1) * beads)
                weight = edge_ref[frame, index * group + part]
                a = (act[:, here].reshape(blocks, SUB, beads) * weight[None]).reshape(hidden, beads)
                s = (slope[:, here].reshape(blocks, SUB, beads) * (weight * jnp.asarray(0.5, BF16))[None]).reshape(hidden, beads)
                kept.append(s)
                act_sum = a if act_sum is None else act_sum + a
                slope_sum = s if slope_sum is None else slope_sum + s
            slope_ref[frame, :, at] = jnp.concatenate(kept, axis=1)
            total_ref[:, lanes] += act_sum.astype(F32)
            slope_total_ref[:, lanes] += slope_sum.astype(F32)
            return carry

        for index in range(degree // group):
            step(index, 0)


def scatter(onehot_ref, slope_ref, cot_gathered, frame, beads, group=8):
    count = slope_ref.shape[2] // beads
    lanes = slice(frame * beads, (frame + 1) * beads)
    wide = jnp.concatenate([cot_gathered[:, lanes]] * group, axis=1)
    total = None
    for index in range(count // group):
        at = slice(index * group * beads, (index + 1) * group * beads)
        part = mul_nt(slope_ref[frame, :, at] * wide, onehot_ref[frame, :, at])
        total = part if total is None else total + part
    return total


def first_kernel(
    hf_ref, hs_ref, onehot_ref, edge_ref, wta_ref, wtb_ref, own_ref, cross_ref, state_ref, select_ref,
    next_ref, first_ref, second_ref, halo_ref, gathered_ref, slope_ref, slope_total_ref,
    total_ref,
):
    halo = read_halo(hf_ref, hs_ref)
    halo_ref[...] = halo
    halo_rows = mul(wta_ref[...], halo).astype(BF16)
    edges(onehot_ref, edge_ref, own_ref[...], halo_rows, cross_ref[...], slope_ref, total_ref, slope_total_ref)
    gathered = total_ref[...].astype(BF16)
    gathered_ref[...] = gathered
    state = (state_ref[...].astype(F32) + mul(wtb_ref[...], gathered)).astype(BF16)
    next_ref[...] = state
    write_halo(first_ref, second_ref, mul(state, select_ref[...]))


def middle_kernel(
    scale,
    hf_ref, hs_ref, onehot_ref, edge_ref, wta_ref, wtc_ref, wtb_ref, wb_ref, state_ref, live_ref, sign_ref, readout_ref,
    energy_ref, grad_readout_ref, cot_ref, first_ref, second_ref, cot_own_ref, cot_halo_ref, cot_cross_ref,
    halo_ref, gathered_ref, cot_low_ref,
    slope_ref, slope_total_ref, total_ref,
):
    last = wb_ref.shape[0] - 1
    beads = edge_ref.shape[3]
    frames = edge_ref.shape[0]
    halo = read_halo(hf_ref, hs_ref)
    halo_ref[...] = halo
    state = state_ref[...]
    own = mul(wta_ref[...], state).astype(BF16)
    cross = mul(wtc_ref[...], state)
    halo_rows = mul(wta_ref[...], halo).astype(BF16)
    edges(onehot_ref, edge_ref, own, halo_rows, cross, slope_ref, total_ref, slope_total_ref)
    gathered = total_ref[...].astype(BF16)
    gathered_ref[...] = gathered
    final = (state.astype(F32) + mul(wtb_ref[...], gathered)).astype(BF16).astype(F32)
    sigmoid = jax.nn.sigmoid(final)
    activated = final * sigmoid
    readout = jnp.concatenate([readout_ref[...]] * frames, axis=1)
    live = live_ref[...]
    sign = sign_ref[...]
    energy = live * jnp.sum(activated * readout, axis=0, keepdims=True)
    for frame in range(frames):
        energy_ref[frame : frame + 1, :] = energy[:, frame * beads : (frame + 1) * beads]
    signs = jnp.broadcast_to(sign, (SUB, sign.shape[1])).astype(BF16)
    grad_readout_ref[...] = mul_nt(signs, activated.astype(BF16)) * scale
    cot = (sign * scale) * readout * (sigmoid * (1.0 + final * (1.0 - sigmoid)))
    cot_ref[...] = cot
    cot_low = cot.astype(BF16)
    cot_low_ref[...] = cot_low
    cot_gathered = mul(wb_ref[last], cot_low)
    cot_cross_ref[...] = (cot_gathered * slope_total_ref[...]).astype(BF16)
    cot_gathered = cot_gathered.astype(BF16)
    cot_halo = None
    for frame in range(frames):
        part = scatter(onehot_ref, slope_ref, cot_gathered, frame, beads)
        cot_own_ref[:, frame * beads : (frame + 1) * beads] = part[:, :beads]
        cot_halo = part[:, beads:] if cot_halo is None else cot_halo + part[:, beads:]
    write_halo(first_ref, second_ref, cot_halo)
    cot_halo_ref[...] = cot_halo.astype(BF16)


def put_slots(slots_ref, me, grads, base=0):
    slots = slots_ref.shape[0]
    rows = grads[0].shape[0] // slots
    for chunk in range(slots):
        slot = jnp.bitwise_xor(me, chunk)
        for number, grad in enumerate(grads):
            start = base + number * rows
            slots_ref[slot, start : start + rows, :] = grad[chunk * rows : (chunk + 1) * rows]


def upper_grads_kernel(
    me_ref, state_ref, halo_ref, gathered_ref, cot_low_ref, cot_own_ref, cot_halo_ref, cot_cross_ref, grad_readout_ref, slots_ref
):
    me = me_ref[0]
    state = state_ref[...]
    grad_a = mul_nt(state, cot_own_ref[...].astype(BF16)) + mul_nt(halo_ref[...], cot_halo_ref[...])
    grad_c = mul_nt(state, cot_cross_ref[...])
    grad_b = mul_nt(gathered_ref[...], cot_low_ref[...])
    row = lax.broadcasted_iota(jnp.int32, (SUB, slots_ref.shape[2]), 0)
    head = jnp.where(row == 0, grad_readout_ref[...], 0.0)
    for slot in range(slots_ref.shape[0]):
        slots_ref[slot, :SUB, :] = head
    put_slots(slots_ref, me, [grad_a, grad_c, grad_b], SUB)


def lower_kernel(
    me_ref, bf_ref, bs_ref, select_ref, cot_own_ref, cot_cross_ref, cot_ref, wa_ref, wc_ref, wb_ref,
    onehot_ref, slope_ref, slope_total_ref, state_ref, halo_ref, gathered_ref, _after,
    slots_ref,
):
    frames = onehot_ref.shape[0]
    beads = cot_ref.shape[1] // frames
    back = read_halo(bf_ref, bs_ref)
    cot_own = (cot_own_ref[...] + mul_nt(back, select_ref[...])).astype(BF16)
    cot = cot_ref[...] + mul(wa_ref[1], cot_own) + mul(wc_ref[1], cot_cross_ref[...])
    cot_low = cot.astype(BF16)
    state = state_ref[...]
    grad_b = mul_nt(gathered_ref[...], cot_low)
    cot_gathered = mul(wb_ref[0], cot_low)
    grad_c = mul_nt(state, (cot_gathered * slope_total_ref[...]).astype(BF16))
    cot_gathered = cot_gathered.astype(BF16)
    cot_halo, grad_a = None, None
    for frame in range(frames):
        lanes = slice(frame * beads, (frame + 1) * beads)
        part = scatter(onehot_ref, slope_ref, cot_gathered, frame, beads)
        here = mul_nt(state[:, lanes], part[:, :beads].astype(BF16))
        grad_a = here if grad_a is None else grad_a + here
        cot_halo = part[:, beads:] if cot_halo is None else cot_halo + part[:, beads:]
    grad_a = grad_a + mul_nt(halo_ref[...], cot_halo.astype(BF16))
    put_slots(slots_ref, me_ref[0], [grad_a, grad_c, grad_b])


def finish_kernel(me_ref, *refs):
    *near, far, wa_ref, wc_ref, wb_ref, readout_ref = refs
    me = me_ref[0]
    count = len(near)
    rows = (far.shape[1] - SUB) // 6
    total = jnp.zeros(readout_ref.shape, F32)
    for slot in range(2 * count):
        source = near[slot] if slot < count else far.at[slot - count]
        chunk = jnp.bitwise_xor(me, slot)
        place = pl.ds(pl.multiple_of(chunk * rows, rows), rows)
        for layer, base in ((1, SUB), (0, SUB + 3 * rows)):
            for number, ref in enumerate((wa_ref, wc_ref, wb_ref)):
                ref[layer, place, :] = source[base + number * rows : base + (number + 1) * rows, :].astype(F32)
        total = jnp.where(chunk == 0, source[:SUB, :].astype(F32)[0], total)
    readout_ref[...] = total


def kernel_call(body, outs, args, scratch=(), flops=0, smem=0, far=0, limit=24):
    spaces = [pltpu.SMEM] * smem + [pltpu.HBM] * far + [pltpu.VMEM] * (len(args) - smem - far)
    args = [pltpu.with_memory_space_constraint(a, pltpu.HBM) if s is pltpu.HBM else a for a, s in zip(args, spaces)]
    return pl.pallas_call(
        body,
        out_shape=outs,
        in_specs=[pl.BlockSpec(memory_space=space) for space in spaces],
        out_specs=jax.tree.map(
            lambda out: pl.BlockSpec(memory_space=pltpu.HBM if getattr(out, "memory_space", None) is pltpu.HBM else pltpu.VMEM), outs
        ),
        scratch_shapes=list(scratch),
        compiler_params=pltpu.CompilerParams(vmem_limit_bytes=limit * MEBI),
        cost_estimate=pl.CostEstimate(flops=flops, bytes_accessed=0, transcendentals=0),
    )(*args)


def near(shape, dtype=BF16):
    return pltpu.VMEM(shape, dtype)


def swapped(value, kind):
    count = lax.axis_size(RING)
    if kind == 0:
        pairs = [(s, s ^ 1) for s in range(count)]
    else:
        pairs = [(s, (s + 1) % count if s % 2 else (s - 1) % count) for s in range(count)]
    return lax.ppermute(value, RING, pairs)


def partner(value, axis, bits):
    return lax.ppermute(value, axis, [(s, s ^ bits) for s in range(lax.axis_size(axis))])


def summed(*terms):
    terms = [term.astype(F32) for term in terms]
    while len(terms) > 1:
        terms = [terms[n] + terms[n + 1] if n + 1 < len(terms) else terms[n] for n in range(0, len(terms), 2)]
    return terms[0].astype(BF16)


def powers(bounds):
    return jnp.clip(jnp.ceil(jnp.log2(jnp.maximum(bounds, 1e-37))), -120.0, 120.0)


def scaled(part):
    count, rows, width = part.shape
    head, body = part[:, :1], part[:, SUB:].reshape(count, 6, -1, width)
    power = powers(jnp.concatenate([jnp.abs(head), jnp.max(jnp.abs(body), axis=2)], axis=1))
    factor = jnp.exp2(-power)
    body = (body * factor[:, 1:, None]).reshape(count, -1, width)
    rest = jnp.zeros((count, SUB - 8, width), F32)
    return jnp.concatenate([head * factor[:, :1], power, rest, body], axis=1).astype(F16)


def restored(sent):
    rows, width = sent.shape
    sent = sent.astype(F32)
    factor = jnp.exp2(sent[1:8])
    body = sent[SUB:].reshape(6, -1, width) * factor[1:, None]
    return jnp.concatenate([sent[:1] * factor[:1], jnp.zeros((SUB - 1, width), F32), body.reshape(-1, width)], axis=0)


def plane(value, x, y):
    rep, dom, tp = (lax.axis_size(a) for a in EVERY)
    flip = (2 * dom * tp if x else 0) + (1 if y else 0)
    return lax.ppermute(value, EVERY, [(s, s ^ flip) for s in range(rep * dom * tp)])


def along_dom(mine):
    count, bit = lax.axis_size("dom"), 1
    while bit < count:
        flips = [bit] if 2 * bit >= count else [bit, 2 * bit, 3 * bit]
        mine = summed(mine, *[partner(mine, "dom", flip) for flip in flips])
        bit *= 4
    return mine


def core_sum(slots):
    return slots[:4] + partner(slots[4:], "rep", 1)


def reduce_parts(parts):
    part = jnp.concatenate(parts, axis=1)
    sent = scaled(part[1:])
    terms = [restored(plane(sent[0], 0, 1)), restored(plane(sent[1], 1, 0)), restored(plane(sent[2], 1, 1))]
    mine = along_dom(summed(part[0], *terms))
    return [mine, plane(mine, 0, 1), plane(mine, 1, 0), plane(mine, 1, 1)]


def local(features, radial, neighbours, halo_lists, slab_counts, frame_labels, w_a, w_c, w_b, readout):
    frames, beads, channels = features.shape
    hidden, layers = w_a.shape[2], w_a.shape[0]
    degree, halo = radial.shape[1], halo_lists.shape[2]
    lanes, halo_lanes = frames * beads, 2 * frames * halo
    rows = beads + halo_lanes
    scale = (2.0 / (frames * lax.axis_size("rep"))) / math.sqrt(beads * lax.axis_size(RING))
    rep = lax.axis_index("rep")
    me = (lax.rem(rep, 2) * 4 + (rep // 2) * 2 + lax.axis_index("tp")).astype(jnp.int32)
    where = jnp.stack([me, lax.rem(lax.axis_index(RING), 2).astype(jnp.int32)])

    half = (channels // 2, halo_lanes)
    state, select, first, second, neigh, weight = kernel_call(
        select_kernel,
        (
            near((channels, lanes)),
            near((lanes, halo_lanes)),
            near(half),
            near(half),
            near(neighbours.shape, jnp.int32),
            near(radial.shape),
        ),
        (where, features, halo_lists, neighbours, radial),
        scratch=[
            pltpu.VMEM(features.shape, BF16),
            pltpu.VMEM(halo_lists.shape, jnp.int32),
            pltpu.SemaphoreType.DMA((4,)),
        ],
        smem=1,
        far=4,
    )
    second, first = swapped(second, 1), swapped(first, 0)
    weights = [near((layers, channels, hidden)), near((layers, channels, hidden)), near((layers, hidden, channels))]
    turned = near((hidden, channels))
    onehot_type = near((frames, rows, degree * beads))
    onehot, edge, wa, wc, wb, readout_near, wta, wtb, own, cross = kernel_call(
        functools.partial(prepare_kernel, halo),
        (
            onehot_type,
            near((frames, degree, SUB, beads)),
            *weights,
            near(readout.shape, F32),
            turned,
            turned,
            near((hidden, lanes)),
            near((hidden, lanes), F32),
        ),
        (where, w_a, w_c, w_b, readout, state, neigh, weight),
        scratch=[
            pltpu.VMEM(neighbours.shape, jnp.int32),
            pltpu.SemaphoreType.DMA((4,)),
        ],
        smem=1,
        far=4,
        flops=2 * 10**9,
    )
    totals = (hidden, lanes)
    edge_slopes = (frames, hidden, degree * beads)
    state1, first, second, halo0, gathered0, slope0, slope_total0 = kernel_call(
        first_kernel,
        (
            near((channels, lanes)),
            near(half),
            near(half),
            near((channels, halo_lanes)),
            near(totals),
            near(edge_slopes),
            near(totals, F32),
        ),
        (first, second, onehot, edge, wta, wtb, own, cross, state, select),
        scratch=[pltpu.VMEM(totals, F32)],
        flops=4 * 10**9,
    )
    wta, wtc, wtb, wide, live, sign = kernel_call(
        later_kernel,
        (turned, turned, turned, near((channels, beads), F32), near((1, lanes), F32), near((1, lanes), F32)),
        (jnp.concatenate([slab_counts[:, 0], frame_labels]), first, wa, wc, wb, readout_near),
        smem=1,
        flops=10**8,
    )
    second, first = swapped(second, 1), swapped(first, 0)
    energy, grad_readout, cot, first, second, cot_own, cot_halo, cot_cross, halo1, gathered1, cot_low1 = kernel_call(
        functools.partial(middle_kernel, scale),
        (
            jax.ShapeDtypeStruct((frames, beads), F32),
            near((SUB, channels), F32),
            near((channels, lanes), F32),
            near(half),
            near(half),
            near(totals, F32),
            near((hidden, halo_lanes)),
            near(totals),
            near((channels, halo_lanes)),
            near(totals),
            near((channels, lanes)),
        ),
        (first, second, onehot, edge, wta, wtc, wtb, wb, state1, live, sign, wide),
        scratch=[pltpu.VMEM(edge_slopes, BF16), pltpu.VMEM(totals, F32), pltpu.VMEM(totals, F32)],
        flops=6 * 10**9,
    )
    second, first = swapped(second, 1), swapped(first, 0)
    chunk = hidden // 8
    upper_slots = kernel_call(
        upper_grads_kernel,
        near((8, SUB + 3 * chunk, channels), F32),
        (where, state1, halo1, gathered1, cot_low1, cot_own, cot_halo, cot_cross, grad_readout),
        smem=1,
        flops=10**9,
    )
    upper_part = core_sum(upper_slots)
    lower_slots = kernel_call(
        lower_kernel,
        near((8, 3 * chunk, channels), F32),
        (
            where, first, second, select, cot_own, cot_cross, cot, wa, wc, wb,
            onehot, slope0, slope_total0, state, halo0, gathered0, upper_slots,
        ),
        smem=1,
        flops=4 * 10**9,
    )
    close = reduce_parts([upper_part, core_sum(lower_slots)])
    far = partner(jnp.stack(close), "rep", 1)
    grad = jax.ShapeDtypeStruct((layers, channels, hidden), F32)
    grad_wa, grad_wc, grad_wb, grad_readout = kernel_call(
        finish_kernel,
        (grad, grad, grad, jax.ShapeDtypeStruct((channels,), F32)),
        (where, *close, far),
        smem=1,
    )
    return grad_wa, grad_wc, grad_wb, grad_readout, energy


def solution(mesh):
    placed = (
        P("rep", RING, None),
        P("rep", None, RING),
        P("rep", None, RING),
        P("rep", None, RING),
        P("rep", RING),
        P("rep"),
        P(),
        P(),
        P(),
        P(),
    )
    return jax.shard_map(
        local,
        mesh=mesh,
        in_specs=placed,
        out_specs=(P(), P(), P(), P(), P("rep", RING)),
        check_vma=False,
    )
```

```python
import functools
import math

import jax
import jax.numpy as jnp
from jax import lax
from jax.experimental import pallas as pl
from jax.experimental.pallas import tpu as pltpu
from jax.sharding import PartitionSpec as P

BF16, F16, F32 = jnp.bfloat16, jnp.float16, jnp.float32
MEBI = 1024 * 1024
SUB = 16
TAIL = 8
RING = ("dom", "tp")
EVERY = ("rep", "dom", "tp")


def mul(a, b):
    return jnp.dot(a, b, preferred_element_type=F32)


def mul_nt(a, b):
    return lax.dot_general(a, b, (((1,), (1,)), ((), ())), preferred_element_type=F32)


def mul_tn(a, b):
    return lax.dot_general(a, b, (((0,), (0,)), ((), ())), preferred_element_type=F32)


def packed_halves(both):
    rows, lanes = both.shape[0] // 2, both.shape[1] // 2
    low, high = both[:rows], both[rows:]
    first = jnp.concatenate([low[:, :lanes], high[:, :lanes]], axis=1)
    second = jnp.concatenate([low[:, lanes:], high[:, lanes:]], axis=1)
    return first, second


def unpacked_halves(first, second):
    lanes = first.shape[1] // 2
    low = jnp.concatenate([first[:, :lanes], second[:, :lanes]], axis=1)
    high = jnp.concatenate([first[:, lanes:], second[:, lanes:]], axis=1)
    return jnp.concatenate([low, high], axis=0)


def send_lanes(even, list_ref, beads):
    parts = []
    for side in range(2):
        for frame in range(list_ref.shape[0]):
            down, up = list_ref[frame, 0:1, :], list_ref[frame, 1:2, :]
            parts.append((jnp.where(even, down, up) if side else jnp.where(even, up, down)) + frame * beads)
    return jnp.concatenate(parts, axis=1)


def write_halo(first_ref, second_ref, both):
    first, second = packed_halves(both)
    first_ref[...] = first.astype(BF16)
    second_ref[...] = second.astype(BF16)


def read_halo(first_ref, second_ref):
    return unpacked_halves(first_ref[...].astype(F32), second_ref[...].astype(F32)).astype(BF16)


def copies_of(pairs, sems):
    copies = [pltpu.make_async_copy(source, target, sems.at[n]) for n, (source, target) in enumerate(pairs)]
    for copy in copies:
        copy.start()
    return copies


def select_kernel(
    where_ref, feat_hbm, list_hbm, neigh_hbm, radial_hbm,
    state_ref, select_ref, first_ref, second_ref, neigh_ref, radial_ref,
    feat_ref, list_ref, sems,
):
    pairs = [(list_hbm, list_ref), (feat_hbm, feat_ref), (neigh_hbm, neigh_ref), (radial_hbm, radial_ref)]
    list_copy, feat_copy, *others = copies_of(pairs, sems)
    list_copy.wait()
    frames, beads, channels = feat_ref.shape
    lanes = frames * beads
    sent = send_lanes(where_ref[1] == 0, list_ref, beads)
    row = lax.broadcasted_iota(jnp.int32, (lanes, sent.shape[1]), 0)
    select = jnp.where(row == sent, 1.0, 0.0).astype(BF16)
    feat_copy.wait()
    state = feat_ref[...].reshape(lanes, channels).astype(F32).T.astype(BF16)
    write_halo(first_ref, second_ref, mul(state, select))
    state_ref[...] = state
    select_ref[...] = select
    for copy in others:
        copy.wait()


def write_onehot(onehot_ref, slots_ref):
    frames, degree, beads = slots_ref.shape
    row = lax.broadcasted_iota(jnp.int32, (onehot_ref.shape[1], beads), 0)
    for frame in range(frames):
        for slot in range(degree):
            hit = row == slots_ref[frame, slot : slot + 1, :]
            onehot_ref[frame, :, slot * beads : (slot + 1) * beads] = jnp.where(hit, 1.0, 0.0).astype(BF16)


def prepare_kernel(
    halo, where_ref, wa_hbm, wc_hbm, wb_hbm, readout_hbm, state_ref, neigh_ref, radial_ref,
    onehot_ref, edge_ref, wa_ref, wc_ref, wb_ref, readout_ref, wta_ref, wtb_ref, own_ref, cross_ref,
    slots_ref, sems,
):
    frames, degree, beads = neigh_ref.shape
    pairs = [(wa_hbm, wa_ref), (wc_hbm, wc_ref), (wb_hbm, wb_ref), (readout_hbm, readout_ref)]
    copies = copies_of(pairs, sems)
    odd = where_ref[1] != 0
    for frame in range(frames):
        neigh = neigh_ref[frame]
        weight = jnp.where(neigh >= 0, radial_ref[frame].astype(F32), 0.0)
        entry = neigh - beads
        upper = entry >= halo
        entry = jnp.where(upper, entry - halo, entry) + (beads + frame * halo)
        upper = jnp.where(upper, 1, 0)
        side = jnp.where(odd, upper, 1 - upper)
        slots_ref[frame] = jnp.where(neigh < beads, neigh, entry + side * (frames * halo))
        for slot in range(degree):
            edge_ref[frame, slot] = jnp.broadcast_to(weight[slot : slot + 1, :], (SUB, beads)).astype(BF16)
    write_onehot(onehot_ref, slots_ref)
    for copy in copies:
        copy.wait()
    turned = wa_ref[0].astype(F32).T.astype(BF16)
    wta_ref[...] = turned
    wtb_ref[...] = wb_ref[0].astype(F32).T.astype(BF16)
    own_ref[...] = mul(turned, state_ref[...]).astype(BF16)
    cross_ref[...] = mul(wc_ref[0].astype(F32).T.astype(BF16), state_ref[...])


def later_kernel(
    frame_ref, state_ref, wa_ref, wc_ref, wb_ref, readout_ref, wta_ref, wtb_ref, own_ref, cross_ref, wide_ref, live_ref, sign_ref
):
    last = wa_ref.shape[0] - 1
    turned_a, turned_c, turned_b = (ref[last].astype(F32).T.astype(BF16) for ref in (wa_ref, wc_ref, wb_ref))
    wta_ref[...] = turned_a
    wtb_ref[...] = turned_b
    own_ref[...] = mul(turned_a, state_ref[...]).astype(BF16)
    cross_ref[...] = mul(turned_c, state_ref[...])
    wide = readout_ref[...].reshape(1, -1)
    beads = wide_ref.shape[1]
    wide_ref[...] = jnp.broadcast_to(wide, (beads, wide.shape[1])).T
    frames = live_ref.shape[1] // beads
    bead = lax.broadcasted_iota(jnp.int32, (1, beads), 1)
    for frame in range(frames):
        live = jnp.where(bead < frame_ref[frame], 1.0, 0.0)
        here = slice(frame * beads, (frame + 1) * beads)
        live_ref[:, here] = live
        sign_ref[:, here] = jnp.where(frame_ref[frames + frame] == 0, live, -live)


def edges(onehot_ref, edge_ref, own, halo, cross, slope_ref, total_ref, slope_total_ref, group=4):
    frames, degree, _, beads = edge_ref.shape
    hidden = own.shape[0]
    blocks = hidden // SUB
    for frame in range(frames):
        lanes = slice(frame * beads, (frame + 1) * beads)
        table = jnp.concatenate([own[:, lanes], halo], axis=1) * jnp.asarray(0.5, BF16)
        half_cross = cross[:, lanes] * 0.5
        wide_cross = jnp.concatenate([half_cross] * group, axis=1)
        total_ref[:, lanes] = jnp.zeros((hidden, beads), F32)
        slope_total_ref[:, lanes] = jnp.zeros((hidden, beads), F32)

        def step(index, carry):
            at = slice(index * group * beads, (index + 1) * group * beads)
            half = (mul(table, onehot_ref[frame, :, at]) + wide_cross).astype(BF16)
            turn = jnp.tanh(half)
            rise = 1 + turn
            rest = 1 + half * (1 - turn)
            act_sum, slope_sum = None, None
            kept = []
            for part in range(group):
                here = slice(part * beads, (part + 1) * beads)
                weight = edge_ref[frame, index * group + part]
                weighted = (rise[:, here].reshape(blocks, SUB, beads) * weight[None]).reshape(hidden, beads)
                a = half[:, here] * weighted
                s = rest[:, here] * weighted
                kept.append(s)
                act_sum = a if act_sum is None else act_sum + a
                slope_sum = s if slope_sum is None else slope_sum + s
            slope_ref[frame, :, at] = jnp.concatenate(kept, axis=1)
            total_ref[:, lanes] += act_sum.astype(F32)
            slope_total_ref[:, lanes] += slope_sum.astype(F32)
            return carry

        for index in range(degree // group):
            step(index, 0)


def scatter(onehot_ref, slope_ref, cot_gathered, frame, beads, group=8):
    count = slope_ref.shape[2] // beads
    lanes = slice(frame * beads, (frame + 1) * beads)
    wide = jnp.concatenate([cot_gathered[:, lanes]] * group, axis=1)
    total = None
    for index in range(count // group):
        at = slice(index * group * beads, (index + 1) * group * beads)
        part = mul_nt(slope_ref[frame, :, at] * wide, onehot_ref[frame, :, at])
        total = part if total is None else total + part
    return total


def first_kernel(
    hs_ref, hf_ref, onehot_ref, edge_ref, wta_ref, wtb_ref, own_ref, cross_ref, state_ref, select_ref,
    next_ref, first_ref, second_ref, halo_ref, gathered_ref, slope_ref, slope_total_ref,
    total_ref,
):
    halo = read_halo(hf_ref, hs_ref)
    halo_ref[...] = halo
    halo_rows = mul(wta_ref[...], halo).astype(BF16)
    edges(onehot_ref, edge_ref, own_ref[...], halo_rows, cross_ref[...], slope_ref, total_ref, slope_total_ref)
    gathered = total_ref[...].astype(BF16)
    gathered_ref[...] = gathered
    state = (state_ref[...].astype(F32) + mul(wtb_ref[...], gathered)).astype(BF16)
    next_ref[...] = state
    write_halo(first_ref, second_ref, mul(state, select_ref[...]))


def middle_kernel(
    scale,
    hs_ref, hf_ref, onehot_ref, edge_ref, wta_ref, wtb_ref, wb_ref, own_ref, cross_ref, state_ref, live_ref, sign_ref, readout_ref,
    energy_ref, grad_readout_ref, cot_ref, first_ref, second_ref, cot_own_ref, cot_halo_ref, cot_cross_ref,
    halo_ref, gathered_ref, cot_low_ref,
    slope_ref, slope_total_ref, total_ref,
):
    last = wb_ref.shape[0] - 1
    beads = edge_ref.shape[3]
    frames = edge_ref.shape[0]
    halo = read_halo(hf_ref, hs_ref)
    halo_ref[...] = halo
    state = state_ref[...]
    halo_rows = mul(wta_ref[...], halo).astype(BF16)
    edges(onehot_ref, edge_ref, own_ref[...], halo_rows, cross_ref[...], slope_ref, total_ref, slope_total_ref)
    gathered = total_ref[...].astype(BF16)
    gathered_ref[...] = gathered
    final = (state.astype(F32) + mul(wtb_ref[...], gathered)).astype(BF16).astype(F32)
    sigmoid = jax.nn.sigmoid(final)
    activated = final * sigmoid
    readout = jnp.concatenate([readout_ref[...]] * frames, axis=1)
    live = live_ref[...]
    sign = sign_ref[...]
    energy = live * jnp.sum(activated * readout, axis=0, keepdims=True)
    for frame in range(frames):
        energy_ref[frame : frame + 1, :] = energy[:, frame * beads : (frame + 1) * beads]
    signs = jnp.broadcast_to(sign, (SUB, sign.shape[1])).astype(BF16)
    grad_readout_ref[...] = mul_nt(signs, activated.astype(BF16)) * scale
    cot = (sign * scale) * readout * (sigmoid * (1.0 + final * (1.0 - sigmoid)))
    cot_ref[...] = cot
    cot_low = cot.astype(BF16)
    cot_low_ref[...] = cot_low
    cot_gathered = mul(wb_ref[last], cot_low) * 0.5
    cot_cross_ref[...] = (cot_gathered * slope_total_ref[...]).astype(BF16)
    cot_gathered = cot_gathered.astype(BF16)
    cot_halo = None
    for frame in range(frames):
        part = scatter(onehot_ref, slope_ref, cot_gathered, frame, beads)
        cot_own_ref[:, frame * beads : (frame + 1) * beads] = part[:, :beads]
        cot_halo = part[:, beads:] if cot_halo is None else cot_halo + part[:, beads:]
    write_halo(first_ref, second_ref, cot_halo)
    cot_halo_ref[...] = cot_halo.astype(BF16)


def put_slots(slots_ref, me, grads):
    slots = slots_ref.shape[0]
    rows = grads[0].shape[0] // slots
    for chunk in range(slots):
        slot = jnp.bitwise_xor(me, chunk)
        for number, grad in enumerate(grads):
            start = number * rows
            slots_ref[slot, start : start + rows, :] = grad[chunk * rows : (chunk + 1) * rows]


def upper_grads_kernel(
    me_ref, state_ref, halo_ref, gathered_ref, cot_low_ref, cot_own_ref, cot_halo_ref, cot_cross_ref, grad_readout_ref,
    cot_ref, wc_ref,
    slots_ref, base_ref,
):
    me = me_ref[0]
    state = state_ref[...]
    grad_a = mul_nt(state, cot_own_ref[...].astype(BF16)) + mul_nt(halo_ref[...], cot_halo_ref[...])
    grad_c = mul_nt(state, cot_cross_ref[...])
    grad_b = mul_nt(gathered_ref[...], cot_low_ref[...])
    row = lax.broadcasted_iota(jnp.int32, (TAIL, slots_ref.shape[2]), 0)
    tail = jnp.where(row == 0, grad_readout_ref[:TAIL], 0.0)
    for slot in range(slots_ref.shape[0]):
        slots_ref[slot, slots_ref.shape[1] - TAIL :, :] = tail
    put_slots(slots_ref, me, [grad_a, grad_c, grad_b])
    base_ref[...] = cot_ref[...] + mul(wc_ref[1], cot_cross_ref[...])


def lower_kernel(
    me_ref, bs_ref, bf_ref, select_ref, cot_own_ref, cot_ref, wa_ref, wb_ref,
    onehot_ref, slope_ref, slope_total_ref, state_ref, halo_ref, gathered_ref,
    slots_ref,
):
    frames = onehot_ref.shape[0]
    beads = cot_ref.shape[1] // frames
    back = read_halo(bf_ref, bs_ref)
    cot_own = (cot_own_ref[...] + mul_nt(back, select_ref[...])).astype(BF16)
    cot = cot_ref[...] + mul(wa_ref[1], cot_own)
    cot_low = cot.astype(BF16)
    state = state_ref[...]
    grad_b = mul_nt(gathered_ref[...], cot_low)
    cot_gathered = mul(wb_ref[0], cot_low) * 0.5
    grad_c = mul_nt(state, (cot_gathered * slope_total_ref[...]).astype(BF16))
    cot_gathered = cot_gathered.astype(BF16)
    cot_halo, grad_a = None, None
    for frame in range(frames):
        lanes = slice(frame * beads, (frame + 1) * beads)
        part = scatter(onehot_ref, slope_ref, cot_gathered, frame, beads)
        here = mul_nt(state[:, lanes], part[:, :beads].astype(BF16))
        grad_a = here if grad_a is None else grad_a + here
        cot_halo = part[:, beads:] if cot_halo is None else cot_halo + part[:, beads:]
    grad_a = grad_a + mul_nt(halo_ref[...], cot_halo.astype(BF16))
    put_slots(slots_ref, me_ref[0], [grad_a, grad_c, grad_b])


def finish_kernel(me_ref, *refs):
    *near, far, wa_ref, wc_ref, wb_ref, readout_ref = refs
    me = me_ref[0]
    count = len(near)
    rows = (far.shape[1] - TAIL) // 6
    total = jnp.zeros(readout_ref.shape, F32)
    for slot in range(2 * count):
        source = near[count - 1 - slot] if slot < count else far.at[2 * count - 1 - slot]
        chunk = jnp.bitwise_xor(me, slot)
        place = pl.ds(pl.multiple_of(chunk * rows, rows), rows)
        for layer, base in ((0, 0), (1, 3 * rows)):
            for number, ref in enumerate((wa_ref, wc_ref, wb_ref)):
                ref[layer, place, :] = source[base + number * rows : base + (number + 1) * rows, :].astype(F32)
        total = jnp.where(chunk == 0, source[6 * rows :, :].astype(F32)[0], total)
    readout_ref[...] = total


def kernel_call(body, outs, args, scratch=(), flops=0, smem=0, far=0, limit=24):
    spaces = [pltpu.SMEM] * smem + [pltpu.HBM] * far + [pltpu.VMEM] * (len(args) - smem - far)
    args = [pltpu.with_memory_space_constraint(a, pltpu.HBM) if s is pltpu.HBM else a for a, s in zip(args, spaces)]
    return pl.pallas_call(
        body,
        out_shape=outs,
        in_specs=[pl.BlockSpec(memory_space=space) for space in spaces],
        out_specs=jax.tree.map(
            lambda out: pl.BlockSpec(memory_space=pltpu.HBM if getattr(out, "memory_space", None) is pltpu.HBM else pltpu.VMEM), outs
        ),
        scratch_shapes=list(scratch),
        compiler_params=pltpu.CompilerParams(vmem_limit_bytes=limit * MEBI),
        cost_estimate=pl.CostEstimate(flops=flops, bytes_accessed=0, transcendentals=0),
    )(*args)


def near(shape, dtype=BF16):
    return pltpu.VMEM(shape, dtype)


def swapped(value, kind):
    count = lax.axis_size(RING)
    if kind == 0:
        pairs = [(s, s ^ 1) for s in range(count)]
    else:
        pairs = [(s, (s + 1) % count if s % 2 else (s - 1) % count) for s in range(count)]
    return lax.ppermute(value, RING, pairs)


def partner(value, axis, bits):
    return lax.ppermute(value, axis, [(s, s ^ bits) for s in range(lax.axis_size(axis))])


def summed(*terms):
    terms = [term.astype(F32) for term in terms]
    while len(terms) > 1:
        terms = [terms[n] + terms[n + 1] if n + 1 < len(terms) else terms[n] for n in range(0, len(terms), 2)]
    return terms[0].astype(BF16)


def powers(bounds):
    return jnp.clip(jnp.ceil(jnp.log2(jnp.maximum(bounds, 1e-37))), -120.0, 120.0)


def scaled(part):
    count, rows, width = part.shape
    body, readout = part[:, :-TAIL].reshape(count, 6, -1, width), part[:, rows - TAIL : rows - TAIL + 1]
    power = powers(jnp.concatenate([jnp.abs(readout), jnp.max(jnp.abs(body), axis=2)], axis=1))
    factor = jnp.exp2(-power)
    body = (body * factor[:, 1:, None]).reshape(count, -1, width)
    return jnp.concatenate([body, readout * factor[:, :1], power], axis=1).astype(F16)


def restored(sent):
    rows, width = sent.shape
    sent = sent.astype(F32)
    factor = jnp.exp2(sent[rows - TAIL + 1 :])
    body = sent[:-TAIL].reshape(6, -1, width) * factor[1:, None]
    readout = sent[rows - TAIL : rows - TAIL + 1] * factor[:1]
    return jnp.concatenate([body.reshape(-1, width), readout, jnp.zeros((TAIL - 1, width), F32)], axis=0)


def plane(value, x, y):
    rep, dom, tp = (lax.axis_size(a) for a in EVERY)
    flip = (2 * dom * tp if x else 0) + (1 if y else 0)
    return lax.ppermute(value, EVERY, [(s, s ^ flip) for s in range(rep * dom * tp)])


def along_dom(mine):
    count, bit = lax.axis_size("dom"), 1
    while bit < count:
        flips = [bit] if 2 * bit >= count else [3 * bit, 2 * bit, bit]
        mine = summed(mine, *[partner(mine, "dom", flip) for flip in flips])
        bit *= 4
    return mine


def core_sum(slots):
    return slots[:4] + partner(slots[4:], "rep", 1)


def reduce_parts(parts):
    part = jnp.concatenate(parts, axis=1)
    sent = scaled(part[1:])
    terms = [restored(plane(sent[0], 0, 1)), restored(plane(sent[1], 1, 0)), restored(plane(sent[2], 1, 1))]
    mine = along_dom(summed(part[0], *terms))
    return [plane(mine, 1, 1), plane(mine, 1, 0), plane(mine, 0, 1), mine]


def local(features, radial, neighbours, halo_lists, slab_counts, frame_labels, w_a, w_c, w_b, readout):
    frames, beads, channels = features.shape
    hidden, layers = w_a.shape[2], w_a.shape[0]
    degree, halo = radial.shape[1], halo_lists.shape[2]
    lanes, halo_lanes = frames * beads, 2 * frames * halo
    rows = beads + halo_lanes
    scale = (2.0 / (frames * lax.axis_size("rep"))) / math.sqrt(beads * lax.axis_size(RING))
    rep = lax.axis_index("rep")
    me = (lax.rem(rep, 2) * 4 + (rep // 2) * 2 + lax.axis_index("tp")).astype(jnp.int32)
    where = jnp.stack([me, lax.rem(lax.axis_index(RING), 2).astype(jnp.int32)])

    half = (channels // 2, halo_lanes)
    state, select, first, second, neigh, weight = kernel_call(
        select_kernel,
        (
            near((channels, lanes)),
            near((lanes, halo_lanes)),
            near(half),
            near(half),
            near(neighbours.shape, jnp.int32),
            near(radial.shape),
        ),
        (where, features, halo_lists, neighbours, radial),
        scratch=[
            pltpu.VMEM(features.shape, BF16),
            pltpu.VMEM(halo_lists.shape, jnp.int32),
            pltpu.SemaphoreType.DMA((4,)),
        ],
        smem=1,
        far=4,
    )
    second, first = swapped(second, 1), swapped(first, 0)
    weights = [near((layers, channels, hidden)), near((layers, channels, hidden)), near((layers, hidden, channels))]
    turned = near((hidden, channels))
    onehot_type = near((frames, rows, degree * beads))
    onehot, edge, wa, wc, wb, readout_near, wta, wtb, own, cross = kernel_call(
        functools.partial(prepare_kernel, halo),
        (
            onehot_type,
            near((frames, degree, SUB, beads)),
            *weights,
            near(readout.shape, F32),
            turned,
            turned,
            near((hidden, lanes)),
            near((hidden, lanes), F32),
        ),
        (where, w_a, w_c, w_b, readout, state, neigh, weight),
        scratch=[
            pltpu.VMEM(neighbours.shape, jnp.int32),
            pltpu.SemaphoreType.DMA((4,)),
        ],
        smem=1,
        far=4,
        flops=2 * 10**9,
    )
    totals = (hidden, lanes)
    edge_slopes = (frames, hidden, degree * beads)
    state1, first, second, halo0, gathered0, slope0, slope_total0 = kernel_call(
        first_kernel,
        (
            near((channels, lanes)),
            near(half),
            near(half),
            near((channels, halo_lanes)),
            near(totals),
            near(edge_slopes),
            near(totals, F32),
        ),
        (second, first, onehot, edge, wta, wtb, own, cross, state, select),
        scratch=[pltpu.VMEM(totals, F32)],
        flops=4 * 10**9,
    )
    wta, wtb, own, cross, wide, live, sign = kernel_call(
        later_kernel,
        (
            turned, turned, near((hidden, lanes)), near((hidden, lanes), F32), near((channels, beads), F32),
            near((1, lanes), F32), near((1, lanes), F32),
        ),
        (jnp.concatenate([slab_counts[:, 0], frame_labels]), state1, wa, wc, wb, readout_near),
        smem=1,
        flops=10**8,
    )
    second, first = swapped(second, 1), swapped(first, 0)
    energy, grad_readout, cot, first, second, cot_own, cot_halo, cot_cross, halo1, gathered1, cot_low1 = kernel_call(
        functools.partial(middle_kernel, scale),
        (
            jax.ShapeDtypeStruct((frames, beads), F32),
            near((SUB, channels), F32),
            near((channels, lanes), F32),
            near(half),
            near(half),
            near(totals, F32),
            near((hidden, halo_lanes)),
            near(totals),
            near((channels, halo_lanes)),
            near(totals),
            near((channels, lanes)),
        ),
        (second, first, onehot, edge, wta, wtb, wb, own, cross, state1, live, sign, wide),
        scratch=[pltpu.VMEM(edge_slopes, BF16), pltpu.VMEM(totals, F32), pltpu.VMEM(totals, F32)],
        flops=6 * 10**9,
    )
    second, first = swapped(second, 1), swapped(first, 0)
    chunk = hidden // 8
    upper_slots, cot = kernel_call(
        upper_grads_kernel,
        (near((8, 3 * chunk + TAIL, channels), F32), near((channels, lanes), F32)),
        (where, state1, halo1, gathered1, cot_low1, cot_own, cot_halo, cot_cross, grad_readout, cot, wc),
        smem=1,
        flops=10**9,
    )
    upper_part = core_sum(upper_slots)
    lower_slots = kernel_call(
        lower_kernel,
        near((8, 3 * chunk, channels), F32),
        (
            where, second, first, select, cot_own, cot, wa, wb,
            onehot, slope0, slope_total0, state, halo0, gathered0,
        ),
        smem=1,
        flops=4 * 10**9,
    )
    close = reduce_parts([core_sum(lower_slots), upper_part])
    far = partner(jnp.stack(close), "rep", 1)
    grad = jax.ShapeDtypeStruct((layers, channels, hidden), F32)
    grad_wa, grad_wc, grad_wb, grad_readout = kernel_call(
        finish_kernel,
        (grad, grad, grad, jax.ShapeDtypeStruct((channels,), F32)),
        (where, *close, far),
        smem=1,
    )
    return grad_wa, grad_wc, grad_wb, grad_readout, energy


def solution(mesh):
    placed = (
        P("rep", RING, None),
        P("rep", None, RING),
        P("rep", None, RING),
        P("rep", None, RING),
        P("rep", RING),
        P("rep"),
        P(),
        P(),
        P(),
        P(),
    )
    return jax.shard_map(
        local,
        mesh=mesh,
        in_specs=placed,
        out_specs=(P(), P(), P(), P(), P("rep", RING)),
        check_vma=False,
    )
```

```python
import functools
import math

import jax
import jax.numpy as jnp
from jax import lax
from jax.experimental import pallas as pl
from jax.experimental.pallas import tpu as pltpu
from jax.sharding import PartitionSpec as P

BF16, F16, F32 = jnp.bfloat16, jnp.float16, jnp.float32
MEBI = 1024 * 1024
SUB = 16
TAIL = 8
RING = ("dom", "tp")
EVERY = ("rep", "dom", "tp")


def mul(a, b):
    return jnp.dot(a, b, preferred_element_type=F32)


def mul_nt(a, b):
    return lax.dot_general(a, b, (((1,), (1,)), ((), ())), preferred_element_type=F32)


def mul_tn(a, b):
    return lax.dot_general(a, b, (((0,), (0,)), ((), ())), preferred_element_type=F32)


def packed_halves(both):
    rows, lanes = both.shape[0] // 2, both.shape[1] // 2
    low, high = both[:rows], both[rows:]
    first = jnp.concatenate([low[:, :lanes], high[:, :lanes]], axis=1)
    second = jnp.concatenate([low[:, lanes:], high[:, lanes:]], axis=1)
    return first, second


def unpacked_halves(first, second):
    lanes = first.shape[1] // 2
    low = jnp.concatenate([first[:, :lanes], second[:, :lanes]], axis=1)
    high = jnp.concatenate([first[:, lanes:], second[:, lanes:]], axis=1)
    return jnp.concatenate([low, high], axis=0)


def send_lanes(even, list_ref, beads):
    parts = []
    for side in range(2):
        for frame in range(list_ref.shape[0]):
            down, up = list_ref[frame, 0:1, :], list_ref[frame, 1:2, :]
            parts.append((jnp.where(even, down, up) if side else jnp.where(even, up, down)) + frame * beads)
    return jnp.concatenate(parts, axis=1)


def write_halo(first_ref, second_ref, both):
    first, second = packed_halves(both)
    first_ref[...] = first.astype(BF16)
    second_ref[...] = second.astype(BF16)


def read_halo(first_ref, second_ref):
    return unpacked_halves(first_ref[...].astype(F32), second_ref[...].astype(F32)).astype(BF16)


def copies_of(pairs, sems):
    copies = [pltpu.make_async_copy(source, target, sems.at[n]) for n, (source, target) in enumerate(pairs)]
    for copy in copies:
        copy.start()
    return copies


def select_kernel(
    where_ref, feat_hbm, list_hbm, neigh_hbm, radial_hbm,
    state_ref, select_ref, first_ref, second_ref, neigh_ref, radial_ref,
    feat_ref, list_ref, sems,
):
    pairs = [(list_hbm, list_ref), (feat_hbm, feat_ref), (neigh_hbm, neigh_ref), (radial_hbm, radial_ref)]
    list_copy, feat_copy, *others = copies_of(pairs, sems)
    list_copy.wait()
    frames, beads, channels = feat_ref.shape
    lanes = frames * beads
    sent = send_lanes(where_ref[1] == 0, list_ref, beads)
    row = lax.broadcasted_iota(jnp.int32, (lanes, sent.shape[1]), 0)
    select = jnp.where(row == sent, 1.0, 0.0).astype(BF16)
    feat_copy.wait()
    state = feat_ref[...].reshape(lanes, channels).astype(F32).T.astype(BF16)
    write_halo(first_ref, second_ref, mul(state, select))
    state_ref[...] = state
    select_ref[...] = select
    for copy in others:
        copy.wait()


def write_onehot(onehot_ref, slots_ref):
    frames, degree, beads = slots_ref.shape
    row = lax.broadcasted_iota(jnp.int32, (onehot_ref.shape[1], beads), 0)
    for frame in range(frames):
        for slot in range(degree):
            hit = row == slots_ref[frame, slot : slot + 1, :]
            onehot_ref[frame, :, slot * beads : (slot + 1) * beads] = jnp.where(hit, 1.0, 0.0).astype(BF16)


def prepare_kernel(
    halo, where_ref, wa_hbm, wc_hbm, wb_hbm, readout_hbm, state_ref, neigh_ref, radial_ref,
    onehot_ref, edge_ref, wa_ref, wc_ref, wb_ref, readout_ref, wta_ref, wtb_ref, own_ref, cross_ref,
    slots_ref, sems,
):
    frames, degree, beads = neigh_ref.shape
    pairs = [(wa_hbm, wa_ref), (wc_hbm, wc_ref), (wb_hbm, wb_ref), (readout_hbm, readout_ref)]
    copies = copies_of(pairs, sems)
    odd = where_ref[1] != 0
    for frame in range(frames):
        neigh = neigh_ref[frame]
        weight = jnp.where(neigh >= 0, radial_ref[frame].astype(F32), 0.0)
        entry = neigh - beads
        upper = entry >= halo
        entry = jnp.where(upper, entry - halo, entry) + (beads + frame * halo)
        upper = jnp.where(upper, 1, 0)
        side = jnp.where(odd, upper, 1 - upper)
        slots_ref[frame] = jnp.where(neigh < beads, neigh, entry + side * (frames * halo))
        for slot in range(degree):
            edge_ref[frame, slot] = jnp.broadcast_to(weight[slot : slot + 1, :], (SUB, beads)).astype(BF16)
    write_onehot(onehot_ref, slots_ref)
    for copy in copies:
        copy.wait()
    turned = wa_ref[0].astype(F32).T.astype(BF16)
    wta_ref[...] = turned
    wtb_ref[...] = wb_ref[0].astype(F32).T.astype(BF16)
    own_ref[...] = mul(turned, state_ref[...]).astype(BF16)
    cross_ref[...] = mul(wc_ref[0].astype(F32).T.astype(BF16), state_ref[...])


def later_kernel(
    frame_ref, state_ref, wa_ref, wc_ref, wb_ref, readout_ref, wta_ref, wtb_ref, own_ref, cross_ref, wide_ref, live_ref, sign_ref
):
    last = wa_ref.shape[0] - 1
    turned_a, turned_c, turned_b = (ref[last].astype(F32).T.astype(BF16) for ref in (wa_ref, wc_ref, wb_ref))
    wta_ref[...] = turned_a
    wtb_ref[...] = turned_b
    own_ref[...] = mul(turned_a, state_ref[...]).astype(BF16)
    cross_ref[...] = mul(turned_c, state_ref[...])
    wide = readout_ref[...].reshape(1, -1)
    beads = wide_ref.shape[1]
    wide_ref[...] = jnp.broadcast_to(wide, (beads, wide.shape[1])).T
    frames = live_ref.shape[1] // beads
    bead = lax.broadcasted_iota(jnp.int32, (1, beads), 1)
    for frame in range(frames):
        live = jnp.where(bead < frame_ref[frame], 1.0, 0.0)
        here = slice(frame * beads, (frame + 1) * beads)
        live_ref[:, here] = live
        sign_ref[:, here] = jnp.where(frame_ref[frames + frame] == 0, live, -live)


def edges(onehot_ref, edge_ref, own, halo, cross, slope_ref, total_ref, slope_total_ref, group=4):
    frames, degree, _, beads = edge_ref.shape
    hidden = own.shape[0]
    blocks = hidden // SUB
    for frame in range(frames):
        lanes = slice(frame * beads, (frame + 1) * beads)
        table = jnp.concatenate([own[:, lanes], halo], axis=1) * jnp.asarray(0.5, BF16)
        half_cross = cross[:, lanes] * 0.5
        wide_cross = jnp.concatenate([half_cross] * group, axis=1)
        total_ref[:, lanes] = jnp.zeros((hidden, beads), F32)
        slope_total_ref[:, lanes] = jnp.zeros((hidden, beads), F32)

        def step(index, carry):
            at = slice(index * group * beads, (index + 1) * group * beads)
            half = (mul(table, onehot_ref[frame, :, at]) + wide_cross).astype(BF16)
            turn = jnp.tanh(half)
            rise = 1 + turn
            rest = 1 + half * (1 - turn)
            act_sum, slope_sum = None, None
            kept = []
            for part in range(group):
                here = slice(part * beads, (part + 1) * beads)
                weight = edge_ref[frame, index * group + part]
                weighted = (rise[:, here].reshape(blocks, SUB, beads) * weight[None]).reshape(hidden, beads)
                a = half[:, here] * weighted
                s = rest[:, here] * weighted
                kept.append(s)
                act_sum = a if act_sum is None else act_sum + a
                slope_sum = s if slope_sum is None else slope_sum + s
            slope_ref[frame, :, at] = jnp.concatenate(kept, axis=1)
            total_ref[:, lanes] += act_sum.astype(F32)
            slope_total_ref[:, lanes] += slope_sum.astype(F32)
            return carry

        for index in range(degree // group):
            step(index, 0)


def scatter(onehot_ref, slope_ref, cot_gathered, frame, beads, group=8):
    count = slope_ref.shape[2] // beads
    lanes = slice(frame * beads, (frame + 1) * beads)
    wide = jnp.concatenate([cot_gathered[:, lanes]] * group, axis=1)
    total = None
    for index in range(count // group):
        at = slice(index * group * beads, (index + 1) * group * beads)
        part = mul_nt(slope_ref[frame, :, at] * wide, onehot_ref[frame, :, at])
        total = part if total is None else total + part
    return total


def first_kernel(
    hs_ref, hf_ref, onehot_ref, edge_ref, wta_ref, wtb_ref, own_ref, cross_ref, state_ref, select_ref,
    next_ref, first_ref, second_ref, halo_ref, gathered_ref, slope_ref, slope_total_ref,
    total_ref,
):
    halo = read_halo(hf_ref, hs_ref)
    halo_ref[...] = halo
    halo_rows = mul(wta_ref[...], halo).astype(BF16)
    edges(onehot_ref, edge_ref, own_ref[...], halo_rows, cross_ref[...], slope_ref, total_ref, slope_total_ref)
    gathered = total_ref[...].astype(BF16)
    gathered_ref[...] = gathered
    state = (state_ref[...].astype(F32) + mul(wtb_ref[...], gathered)).astype(BF16)
    next_ref[...] = state
    write_halo(first_ref, second_ref, mul(state, select_ref[...]))


def middle_kernel(
    scale,
    hs_ref, hf_ref, onehot_ref, edge_ref, wta_ref, wtb_ref, wb_ref, own_ref, cross_ref, state_ref, live_ref, sign_ref, readout_ref,
    energy_ref, grad_readout_ref, cot_ref, first_ref, second_ref, cot_own_ref, cot_halo_ref, cot_cross_ref,
    halo_ref, gathered_ref, cot_low_ref,
    slope_ref, slope_total_ref, total_ref,
):
    last = wb_ref.shape[0] - 1
    beads = edge_ref.shape[3]
    frames = edge_ref.shape[0]
    halo = read_halo(hf_ref, hs_ref)
    halo_ref[...] = halo
    state = state_ref[...]
    halo_rows = mul(wta_ref[...], halo).astype(BF16)
    edges(onehot_ref, edge_ref, own_ref[...], halo_rows, cross_ref[...], slope_ref, total_ref, slope_total_ref)
    gathered = total_ref[...].astype(BF16)
    gathered_ref[...] = gathered
    final = (state.astype(F32) + mul(wtb_ref[...], gathered)).astype(BF16).astype(F32)
    sigmoid = jax.nn.sigmoid(final)
    activated = final * sigmoid
    readout = jnp.concatenate([readout_ref[...]] * frames, axis=1)
    live = live_ref[...]
    sign = sign_ref[...]
    energy = live * jnp.sum(activated * readout, axis=0, keepdims=True)
    for frame in range(frames):
        energy_ref[frame : frame + 1, :] = energy[:, frame * beads : (frame + 1) * beads]
    signs = jnp.broadcast_to(sign, (SUB, sign.shape[1])).astype(BF16)
    grad_readout_ref[...] = mul_nt(signs, activated.astype(BF16)) * scale
    cot = (sign * scale) * readout * (sigmoid * (1.0 + final * (1.0 - sigmoid)))
    cot_ref[...] = cot
    cot_low = cot.astype(BF16)
    cot_low_ref[...] = cot_low
    cot_gathered = mul(wb_ref[last], cot_low) * 0.5
    cot_cross_ref[...] = (cot_gathered * slope_total_ref[...]).astype(BF16)
    cot_gathered = cot_gathered.astype(BF16)
    cot_halo = None
    for frame in range(frames):
        part = scatter(onehot_ref, slope_ref, cot_gathered, frame, beads)
        cot_own_ref[:, frame * beads : (frame + 1) * beads] = part[:, :beads]
        cot_halo = part[:, beads:] if cot_halo is None else cot_halo + part[:, beads:]
    write_halo(first_ref, second_ref, cot_halo)
    cot_halo_ref[...] = cot_halo.astype(BF16)


def put_slots(slots_ref, me, grads):
    slots = slots_ref.shape[0]
    rows = grads[0].shape[0] // slots
    for chunk in range(slots):
        slot = jnp.bitwise_xor(me, chunk)
        for number, grad in enumerate(grads):
            start = number * rows
            slots_ref[slot, start : start + rows, :] = grad[chunk * rows : (chunk + 1) * rows]


def upper_grads_kernel(
    me_ref, state_ref, halo_ref, gathered_ref, cot_low_ref, cot_own_ref, cot_halo_ref, cot_cross_ref, grad_readout_ref,
    cot_ref, wc_ref,
    slots_ref, base_ref,
):
    me = me_ref[0]
    state = state_ref[...]
    grad_a = mul_nt(state, cot_own_ref[...].astype(BF16)) + mul_nt(halo_ref[...], cot_halo_ref[...])
    grad_c = mul_nt(state, cot_cross_ref[...])
    grad_b = mul_nt(gathered_ref[...], cot_low_ref[...])
    row = lax.broadcasted_iota(jnp.int32, (TAIL, slots_ref.shape[2]), 0)
    tail = jnp.where(row == 0, grad_readout_ref[:TAIL], 0.0)
    for slot in range(slots_ref.shape[0]):
        slots_ref[slot, slots_ref.shape[1] - TAIL :, :] = tail
    put_slots(slots_ref, me, [grad_a, grad_c, grad_b])
    base_ref[...] = cot_ref[...] + mul(wc_ref[1], cot_cross_ref[...])


def lower_kernel(
    me_ref, bf_ref, bs_ref, select_ref, cot_own_ref, cot_ref, wa_ref, wb_ref,
    onehot_ref, slope_ref, slope_total_ref, state_ref, halo_ref, gathered_ref,
    slots_ref,
):
    frames = onehot_ref.shape[0]
    beads = cot_ref.shape[1] // frames
    back = read_halo(bf_ref, bs_ref)
    cot_own = (cot_own_ref[...] + mul_nt(back, select_ref[...])).astype(BF16)
    cot = cot_ref[...] + mul(wa_ref[1], cot_own)
    cot_low = cot.astype(BF16)
    state = state_ref[...]
    grad_b = mul_nt(gathered_ref[...], cot_low)
    cot_gathered = mul(wb_ref[0], cot_low) * 0.5
    grad_c = mul_nt(state, (cot_gathered * slope_total_ref[...]).astype(BF16))
    cot_gathered = cot_gathered.astype(BF16)
    cot_halo, grad_a = None, None
    for frame in range(frames):
        lanes = slice(frame * beads, (frame + 1) * beads)
        part = scatter(onehot_ref, slope_ref, cot_gathered, frame, beads)
        here = mul_nt(state[:, lanes], part[:, :beads].astype(BF16))
        grad_a = here if grad_a is None else grad_a + here
        cot_halo = part[:, beads:] if cot_halo is None else cot_halo + part[:, beads:]
    grad_a = grad_a + mul_nt(halo_ref[...], cot_halo.astype(BF16))
    put_slots(slots_ref, me_ref[0], [grad_a, grad_c, grad_b])


def finish_kernel(me_ref, *refs):
    *sources, wa_ref, wc_ref, wb_ref, readout_ref = refs
    me = me_ref[0]
    count = len(sources) // 2
    rows = (sources[0].shape[0] - TAIL) // 6
    total = jnp.zeros(readout_ref.shape, F32)
    for slot in range(2 * count):
        source = sources[slot ^ (count - 1)]
        chunk = jnp.bitwise_xor(me, slot)
        place = pl.ds(pl.multiple_of(chunk * rows, rows), rows)
        for layer, base in ((0, 0), (1, 3 * rows)):
            for number, ref in enumerate((wa_ref, wc_ref, wb_ref)):
                ref[layer, place, :] = source[base + number * rows : base + (number + 1) * rows, :].astype(F32)
        total = jnp.where(chunk == 0, source[6 * rows :, :].astype(F32)[0], total)
    readout_ref[...] = total


def kernel_call(body, outs, args, scratch=(), flops=0, smem=0, far=0, limit=24):
    spaces = [pltpu.SMEM] * smem + [pltpu.HBM] * far + [pltpu.VMEM] * (len(args) - smem - far)
    args = [pltpu.with_memory_space_constraint(a, pltpu.HBM) if s is pltpu.HBM else a for a, s in zip(args, spaces)]
    return pl.pallas_call(
        body,
        out_shape=outs,
        in_specs=[pl.BlockSpec(memory_space=space) for space in spaces],
        out_specs=jax.tree.map(
            lambda out: pl.BlockSpec(memory_space=pltpu.HBM if getattr(out, "memory_space", None) is pltpu.HBM else pltpu.VMEM), outs
        ),
        scratch_shapes=list(scratch),
        compiler_params=pltpu.CompilerParams(vmem_limit_bytes=limit * MEBI),
        cost_estimate=pl.CostEstimate(flops=flops, bytes_accessed=0, transcendentals=0),
    )(*args)


def near(shape, dtype=BF16):
    return pltpu.VMEM(shape, dtype)


def swapped(value, kind):
    count = lax.axis_size(RING)
    if kind == 0:
        pairs = [(s, s ^ 1) for s in range(count)]
    else:
        pairs = [(s, (s + 1) % count if s % 2 else (s - 1) % count) for s in range(count)]
    return lax.ppermute(value, RING, pairs)


def partner(value, axis, bits):
    return lax.ppermute(value, axis, [(s, s ^ bits) for s in range(lax.axis_size(axis))])


def summed(*terms):
    terms = [term.astype(F32) for term in terms]
    while len(terms) > 1:
        terms = [terms[n] + terms[n + 1] if n + 1 < len(terms) else terms[n] for n in range(0, len(terms), 2)]
    return terms[0].astype(BF16)


def powers(bounds):
    return jnp.clip(jnp.ceil(jnp.log2(jnp.maximum(bounds, 1e-37))), -120.0, 120.0)


def scaled(part):
    count, rows, width = part.shape
    body, readout = part[:, :-TAIL].reshape(count, 6, -1, width), part[:, rows - TAIL : rows - TAIL + 1]
    power = powers(jnp.concatenate([jnp.abs(readout), jnp.max(jnp.abs(body), axis=2)], axis=1))
    factor = jnp.exp2(-power)
    body = (body * factor[:, 1:, None]).reshape(count, -1, width)
    return jnp.concatenate([body, readout * factor[:, :1], power], axis=1).astype(F16)


def restored(sent):
    rows, width = sent.shape
    sent = sent.astype(F32)
    factor = jnp.exp2(sent[rows - TAIL + 1 :])
    body = sent[:-TAIL].reshape(6, -1, width) * factor[1:, None]
    readout = sent[rows - TAIL : rows - TAIL + 1] * factor[:1]
    return jnp.concatenate([body.reshape(-1, width), readout, jnp.zeros((TAIL - 1, width), F32)], axis=0)


def plane(value, x, y):
    rep, dom, tp = (lax.axis_size(a) for a in EVERY)
    flip = (2 * dom * tp if x else 0) + (1 if y else 0)
    return lax.ppermute(value, EVERY, [(s, s ^ flip) for s in range(rep * dom * tp)])


def along_dom(mine):
    count, bit = lax.axis_size("dom"), 1
    while bit < count:
        flips = [bit] if 2 * bit >= count else [3 * bit, 2 * bit, bit]
        mine = summed(mine, *[partner(mine, "dom", flip) for flip in flips])
        bit *= 4
    return mine


def core_sum(slots):
    return slots[:4] + partner(slots[4:], "rep", 1)


def reduce_parts(parts):
    part = jnp.concatenate(parts, axis=1)
    sent = scaled(part[1:])
    terms = [restored(plane(sent[0], 0, 1)), restored(plane(sent[1], 1, 0)), restored(plane(sent[2], 1, 1))]
    mine = along_dom(summed(part[0], *terms))
    return [plane(mine, 1, 1), plane(mine, 1, 0), plane(mine, 0, 1), mine]


def local(features, radial, neighbours, halo_lists, slab_counts, frame_labels, w_a, w_c, w_b, readout):
    frames, beads, channels = features.shape
    hidden, layers = w_a.shape[2], w_a.shape[0]
    degree, halo = radial.shape[1], halo_lists.shape[2]
    lanes, halo_lanes = frames * beads, 2 * frames * halo
    rows = beads + halo_lanes
    scale = (2.0 / (frames * lax.axis_size("rep"))) / math.sqrt(beads * lax.axis_size(RING))
    rep = lax.axis_index("rep")
    me = (lax.rem(rep, 2) * 4 + (rep // 2) * 2 + lax.axis_index("tp")).astype(jnp.int32)
    where = jnp.stack([me, lax.rem(lax.axis_index(RING), 2).astype(jnp.int32)])

    half = (channels // 2, halo_lanes)
    state, select, first, second, neigh, weight = kernel_call(
        select_kernel,
        (
            near((channels, lanes)),
            near((lanes, halo_lanes)),
            near(half),
            near(half),
            near(neighbours.shape, jnp.int32),
            near(radial.shape),
        ),
        (where, features, halo_lists, neighbours, radial),
        scratch=[
            pltpu.VMEM(features.shape, BF16),
            pltpu.VMEM(halo_lists.shape, jnp.int32),
            pltpu.SemaphoreType.DMA((4,)),
        ],
        smem=1,
        far=4,
    )
    second, first = swapped(second, 1), swapped(first, 0)
    weights = [near((layers, channels, hidden)), near((layers, channels, hidden)), near((layers, hidden, channels))]
    turned = near((hidden, channels))
    onehot_type = near((frames, rows, degree * beads))
    onehot, edge, wa, wc, wb, readout_near, wta, wtb, own, cross = kernel_call(
        functools.partial(prepare_kernel, halo),
        (
            onehot_type,
            near((frames, degree, SUB, beads)),
            *weights,
            near(readout.shape, F32),
            turned,
            turned,
            near((hidden, lanes)),
            near((hidden, lanes), F32),
        ),
        (where, w_a, w_c, w_b, readout, state, neigh, weight),
        scratch=[
            pltpu.VMEM(neighbours.shape, jnp.int32),
            pltpu.SemaphoreType.DMA((4,)),
        ],
        smem=1,
        far=4,
        flops=2 * 10**9,
    )
    totals = (hidden, lanes)
    edge_slopes = (frames, hidden, degree * beads)
    state1, first, second, halo0, gathered0, slope0, slope_total0 = kernel_call(
        first_kernel,
        (
            near((channels, lanes)),
            near(half),
            near(half),
            near((channels, halo_lanes)),
            near(totals),
            near(edge_slopes),
            near(totals, F32),
        ),
        (second, first, onehot, edge, wta, wtb, own, cross, state, select),
        scratch=[pltpu.VMEM(totals, F32)],
        flops=4 * 10**9,
    )
    wta, wtb, own, cross, wide, live, sign = kernel_call(
        later_kernel,
        (
            turned, turned, near((hidden, lanes)), near((hidden, lanes), F32), near((channels, beads), F32),
            near((1, lanes), F32), near((1, lanes), F32),
        ),
        (jnp.concatenate([slab_counts[:, 0], frame_labels]), state1, wa, wc, wb, readout_near),
        smem=1,
        flops=10**8,
    )
    second, first = swapped(second, 1), swapped(first, 0)
    energy, grad_readout, cot, first, second, cot_own, cot_halo, cot_cross, halo1, gathered1, cot_low1 = kernel_call(
        functools.partial(middle_kernel, scale),
        (
            jax.ShapeDtypeStruct((frames, beads), F32),
            near((SUB, channels), F32),
            near((channels, lanes), F32),
            near(half),
            near(half),
            near(totals, F32),
            near((hidden, halo_lanes)),
            near(totals),
            near((channels, halo_lanes)),
            near(totals),
            near((channels, lanes)),
        ),
        (second, first, onehot, edge, wta, wtb, wb, own, cross, state1, live, sign, wide),
        scratch=[pltpu.VMEM(edge_slopes, BF16), pltpu.VMEM(totals, F32), pltpu.VMEM(totals, F32)],
        flops=6 * 10**9,
    )
    second, first = swapped(second, 1), swapped(first, 0)
    chunk = hidden // 8
    upper_slots, cot = kernel_call(
        upper_grads_kernel,
        (near((8, 3 * chunk + TAIL, channels), F32), near((channels, lanes), F32)),
        (where, state1, halo1, gathered1, cot_low1, cot_own, cot_halo, cot_cross, grad_readout, cot, wc),
        smem=1,
        flops=10**8,
    )
    upper_part = core_sum(upper_slots)
    lower_slots = kernel_call(
        lower_kernel,
        near((8, 3 * chunk, channels), F32),
        (
            where, first, second, select, cot_own, cot, wa, wb,
            onehot, slope0, slope_total0, state, halo0, gathered0,
        ),
        smem=1,
        flops=4 * 10**9,
    )
    close = reduce_parts([core_sum(lower_slots), upper_part])
    far = [partner(value, "rep", 1) for value in close]
    grad = jax.ShapeDtypeStruct((layers, channels, hidden), F32)
    grad_wa, grad_wc, grad_wb, grad_readout = kernel_call(
        finish_kernel,
        (grad, grad, grad, jax.ShapeDtypeStruct((channels,), F32)),
        (where, *close, *far),
        smem=1,
    )
    return grad_wa, grad_wc, grad_wb, grad_readout, energy


def solution(mesh):
    placed = (
        P("rep", RING, None),
        P("rep", None, RING),
        P("rep", None, RING),
        P("rep", None, RING),
        P("rep", RING),
        P("rep"),
        P(),
        P(),
        P(),
        P(),
    )
    return jax.shard_map(
        local,
        mesh=mesh,
        in_specs=placed,
        out_specs=(P(), P(), P(), P(), P("rep", RING)),
        check_vma=False,
    )
```

```python
import functools
import math

import jax
import jax.numpy as jnp
from jax import lax
from jax.experimental import pallas as pl
from jax.experimental.pallas import tpu as pltpu
from jax.sharding import PartitionSpec as P

BF16, F16, F32 = jnp.bfloat16, jnp.float16, jnp.float32
MEBI = 1024 * 1024
SUB = 16
TAIL = 8
RING = ("dom", "tp")
EVERY = ("rep", "dom", "tp")


def mul(a, b):
    return jnp.dot(a, b, preferred_element_type=F32)


def mul_nt(a, b):
    return lax.dot_general(a, b, (((1,), (1,)), ((), ())), preferred_element_type=F32)


def mul_tn(a, b):
    return lax.dot_general(a, b, (((0,), (0,)), ((), ())), preferred_element_type=F32)


def packed_halves(both):
    rows, lanes = both.shape[0] // 2, both.shape[1] // 2
    low, high = both[:rows], both[rows:]
    first = jnp.concatenate([low[:, :lanes], high[:, :lanes]], axis=1)
    second = jnp.concatenate([low[:, lanes:], high[:, lanes:]], axis=1)
    return first, second


def unpacked_halves(first, second):
    lanes = first.shape[1] // 2
    low = jnp.concatenate([first[:, :lanes], second[:, :lanes]], axis=1)
    high = jnp.concatenate([first[:, lanes:], second[:, lanes:]], axis=1)
    return jnp.concatenate([low, high], axis=0)


def send_lanes(even, list_ref, beads):
    parts = []
    for side in range(2):
        for frame in range(list_ref.shape[0]):
            down, up = list_ref[frame, 0:1, :], list_ref[frame, 1:2, :]
            parts.append((jnp.where(even, down, up) if side else jnp.where(even, up, down)) + frame * beads)
    return jnp.concatenate(parts, axis=1)


def write_halo(first_ref, second_ref, both):
    first, second = packed_halves(both)
    first_ref[...] = first.astype(BF16)
    second_ref[...] = second.astype(BF16)


def read_halo(first_ref, second_ref):
    return unpacked_halves(first_ref[...].astype(F32), second_ref[...].astype(F32)).astype(BF16)


def copies_of(pairs, sems):
    copies = [pltpu.make_async_copy(source, target, sems.at[n]) for n, (source, target) in enumerate(pairs)]
    for copy in copies:
        copy.start()
    return copies


def select_kernel(
    where_ref, feat_hbm, list_hbm, neigh_hbm, radial_hbm,
    state_ref, select_ref, first_ref, second_ref, neigh_ref, radial_ref,
    feat_ref, list_ref, sems,
):
    pairs = [(list_hbm, list_ref), (feat_hbm, feat_ref), (neigh_hbm, neigh_ref), (radial_hbm, radial_ref)]
    list_copy, feat_copy, *others = copies_of(pairs, sems)
    list_copy.wait()
    frames, beads, channels = feat_ref.shape
    lanes = frames * beads
    sent = send_lanes(where_ref[1] == 0, list_ref, beads)
    row = lax.broadcasted_iota(jnp.int32, (lanes, sent.shape[1]), 0)
    select = jnp.where(row == sent, 1.0, 0.0).astype(BF16)
    feat_copy.wait()
    state = feat_ref[...].reshape(lanes, channels).astype(F32).T.astype(BF16)
    write_halo(first_ref, second_ref, mul(state, select))
    state_ref[...] = state
    select_ref[...] = select
    for copy in others:
        copy.wait()


def write_onehot(onehot_ref, slots_ref):
    frames, degree, beads = slots_ref.shape
    row = lax.broadcasted_iota(jnp.int32, (onehot_ref.shape[1], beads), 0)
    for frame in range(frames):
        for slot in range(degree):
            hit = row == slots_ref[frame, slot : slot + 1, :]
            onehot_ref[frame, :, slot * beads : (slot + 1) * beads] = jnp.where(hit, 1.0, 0.0).astype(BF16)


def prepare_kernel(
    halo, where_ref, wa_hbm, wc_hbm, wb_hbm, readout_hbm, state_ref, neigh_ref, radial_ref,
    onehot_ref, edge_ref, wa_ref, wc_ref, wb_ref, readout_ref, wta_ref, wtb_ref, own_ref, cross_ref,
    slots_ref, sems,
):
    frames, degree, beads = neigh_ref.shape
    pairs = [(wa_hbm, wa_ref), (wc_hbm, wc_ref), (wb_hbm, wb_ref), (readout_hbm, readout_ref)]
    copies = copies_of(pairs, sems)
    odd = where_ref[1] != 0
    for frame in range(frames):
        neigh = neigh_ref[frame]
        weight = jnp.where(neigh >= 0, radial_ref[frame].astype(F32), 0.0)
        entry = neigh - beads
        upper = entry >= halo
        entry = jnp.where(upper, entry - halo, entry) + (beads + frame * halo)
        upper = jnp.where(upper, 1, 0)
        side = jnp.where(odd, upper, 1 - upper)
        slots_ref[frame] = jnp.where(neigh < beads, neigh, entry + side * (frames * halo))
        for slot in range(degree):
            edge_ref[frame, slot] = jnp.broadcast_to(weight[slot : slot + 1, :], (SUB, beads)).astype(BF16)
    write_onehot(onehot_ref, slots_ref)
    for copy in copies:
        copy.wait()
    turned = wa_ref[0].astype(F32).T.astype(BF16)
    wta_ref[...] = turned
    wtb_ref[...] = wb_ref[0].astype(F32).T.astype(BF16)
    own_ref[...] = mul(turned, state_ref[...]).astype(BF16)
    cross_ref[...] = mul(wc_ref[0].astype(F32).T.astype(BF16), state_ref[...])


def later_kernel(
    frame_ref, state_ref, wa_ref, wc_ref, wb_ref, readout_ref, wta_ref, wtb_ref, own_ref, cross_ref, wide_ref, live_ref, sign_ref
):
    last = wa_ref.shape[0] - 1
    turned_a, turned_c, turned_b = (ref[last].astype(F32).T.astype(BF16) for ref in (wa_ref, wc_ref, wb_ref))
    wta_ref[...] = turned_a
    wtb_ref[...] = turned_b
    own_ref[...] = mul(turned_a, state_ref[...]).astype(BF16)
    cross_ref[...] = mul(turned_c, state_ref[...])
    wide = readout_ref[...].reshape(1, -1)
    beads = wide_ref.shape[1]
    wide_ref[...] = jnp.broadcast_to(wide, (beads, wide.shape[1])).T
    frames = live_ref.shape[1] // beads
    bead = lax.broadcasted_iota(jnp.int32, (1, beads), 1)
    for frame in range(frames):
        live = jnp.where(bead < frame_ref[frame], 1.0, 0.0)
        here = slice(frame * beads, (frame + 1) * beads)
        live_ref[:, here] = live
        sign_ref[:, here] = jnp.where(frame_ref[frames + frame] == 0, live, -live)


def edges(onehot_ref, edge_ref, own, halo, cross, slope_ref, total_ref, slope_total_ref, group=4):
    frames, degree, _, beads = edge_ref.shape
    hidden = own.shape[0]
    blocks = hidden // SUB
    for frame in range(frames):
        lanes = slice(frame * beads, (frame + 1) * beads)
        table = jnp.concatenate([own[:, lanes], halo], axis=1) * jnp.asarray(0.5, BF16)
        half_cross = cross[:, lanes] * 0.5
        wide_cross = jnp.concatenate([half_cross] * group, axis=1)
        total_ref[:, lanes] = jnp.zeros((hidden, beads), F32)
        slope_total_ref[:, lanes] = jnp.zeros((hidden, beads), F32)

        def step(index, carry):
            at = slice(index * group * beads, (index + 1) * group * beads)
            half = (mul(table, onehot_ref[frame, :, at]) + wide_cross).astype(BF16)
            turn = jnp.tanh(half)
            rise = 1 + turn
            rest = 1 + half * (1 - turn)
            act_sum, slope_sum = None, None
            kept = []
            for part in range(group):
                here = slice(part * beads, (part + 1) * beads)
                weight = edge_ref[frame, index * group + part]
                weighted = (rise[:, here].reshape(blocks, SUB, beads) * weight[None]).reshape(hidden, beads)
                a = half[:, here] * weighted
                s = rest[:, here] * weighted
                kept.append(s)
                act_sum = a if act_sum is None else act_sum + a
                slope_sum = s if slope_sum is None else slope_sum + s
            slope_ref[frame, :, at] = jnp.concatenate(kept, axis=1)
            total_ref[:, lanes] += act_sum.astype(F32)
            slope_total_ref[:, lanes] += slope_sum.astype(F32)
            return carry

        for index in range(degree // group):
            step(index, 0)


def scatter(onehot_ref, slope_ref, cot_gathered, frame, beads, group=8):
    count = slope_ref.shape[2] // beads
    lanes = slice(frame * beads, (frame + 1) * beads)
    wide = jnp.concatenate([cot_gathered[:, lanes]] * group, axis=1)
    total = None
    for index in range(count // group):
        at = slice(index * group * beads, (index + 1) * group * beads)
        part = mul_nt(slope_ref[frame, :, at] * wide, onehot_ref[frame, :, at])
        total = part if total is None else total + part
    return total


def first_kernel(
    hs_ref, hf_ref, onehot_ref, edge_ref, wta_ref, wtb_ref, own_ref, cross_ref, state_ref, select_ref,
    next_ref, first_ref, second_ref, halo_ref, gathered_ref, slope_ref, slope_total_ref,
    total_ref,
):
    halo = read_halo(hf_ref, hs_ref)
    halo_ref[...] = halo
    halo_rows = mul(wta_ref[...], halo).astype(BF16)
    edges(onehot_ref, edge_ref, own_ref[...], halo_rows, cross_ref[...], slope_ref, total_ref, slope_total_ref)
    gathered = total_ref[...].astype(BF16)
    gathered_ref[...] = gathered
    state = (state_ref[...].astype(F32) + mul(wtb_ref[...], gathered)).astype(BF16)
    next_ref[...] = state
    write_halo(first_ref, second_ref, mul(state, select_ref[...]))


def middle_kernel(
    scale,
    hs_ref, hf_ref, onehot_ref, edge_ref, wta_ref, wtb_ref, wb_ref, own_ref, cross_ref, state_ref, live_ref, sign_ref, readout_ref,
    energy_ref, grad_readout_ref, cot_ref, first_ref, second_ref, cot_own_ref, cot_halo_ref, cot_cross_ref,
    halo_ref, gathered_ref, cot_low_ref,
    slope_ref, slope_total_ref, total_ref,
):
    last = wb_ref.shape[0] - 1
    beads = edge_ref.shape[3]
    frames = edge_ref.shape[0]
    halo = read_halo(hf_ref, hs_ref)
    halo_ref[...] = halo
    state = state_ref[...]
    halo_rows = mul(wta_ref[...], halo).astype(BF16)
    edges(onehot_ref, edge_ref, own_ref[...], halo_rows, cross_ref[...], slope_ref, total_ref, slope_total_ref)
    gathered = total_ref[...].astype(BF16)
    gathered_ref[...] = gathered
    final = (state.astype(F32) + mul(wtb_ref[...], gathered)).astype(BF16).astype(F32)
    sigmoid = jax.nn.sigmoid(final)
    activated = final * sigmoid
    readout = jnp.concatenate([readout_ref[...]] * frames, axis=1)
    live = live_ref[...]
    sign = sign_ref[...]
    energy = live * jnp.sum(activated * readout, axis=0, keepdims=True)
    for frame in range(frames):
        energy_ref[frame : frame + 1, :] = energy[:, frame * beads : (frame + 1) * beads]
    signs = jnp.broadcast_to(sign, (SUB, sign.shape[1])).astype(BF16)
    grad_readout_ref[...] = mul_nt(signs, activated.astype(BF16)) * scale
    cot = (sign * scale) * readout * (sigmoid * (1.0 + final * (1.0 - sigmoid)))
    cot_ref[...] = cot
    cot_low = cot.astype(BF16)
    cot_low_ref[...] = cot_low
    cot_gathered = mul(wb_ref[last], cot_low) * 0.5
    cot_cross_ref[...] = (cot_gathered * slope_total_ref[...]).astype(BF16)
    cot_gathered = cot_gathered.astype(BF16)
    cot_halo = None
    for frame in range(frames):
        part = scatter(onehot_ref, slope_ref, cot_gathered, frame, beads)
        cot_own_ref[:, frame * beads : (frame + 1) * beads] = part[:, :beads]
        cot_halo = part[:, beads:] if cot_halo is None else cot_halo + part[:, beads:]
    write_halo(first_ref, second_ref, cot_halo)
    cot_halo_ref[...] = cot_halo.astype(BF16)


def put_slots(slots_ref, me, grads):
    slots = slots_ref.shape[0]
    rows = grads[0].shape[0] // slots
    for chunk in range(slots):
        slot = jnp.bitwise_xor(me, chunk)
        for number, grad in enumerate(grads):
            start = number * rows
            slots_ref[slot, start : start + rows, :] = grad[chunk * rows : (chunk + 1) * rows]


def upper_grads_kernel(
    me_ref, state_ref, halo_ref, gathered_ref, cot_low_ref, cot_own_ref, cot_halo_ref, cot_cross_ref, grad_readout_ref,
    cot_ref, wc_ref,
    slots_ref, base_ref,
):
    me = me_ref[0]
    state = state_ref[...]
    grad_a = mul_nt(state, cot_own_ref[...].astype(BF16)) + mul_nt(halo_ref[...], cot_halo_ref[...])
    grad_c = mul_nt(state, cot_cross_ref[...])
    grad_b = mul_nt(gathered_ref[...], cot_low_ref[...])
    row = lax.broadcasted_iota(jnp.int32, (TAIL, slots_ref.shape[2]), 0)
    tail = jnp.where(row == 0, grad_readout_ref[:TAIL], 0.0)
    for slot in range(slots_ref.shape[0]):
        slots_ref[slot, slots_ref.shape[1] - TAIL :, :] = tail
    put_slots(slots_ref, me, [grad_a, grad_c, grad_b])
    base_ref[...] = cot_ref[...] + mul(wc_ref[1], cot_cross_ref[...])


def lower_kernel(
    me_ref, bf_ref, bs_ref, select_ref, cot_own_ref, cot_ref, wa_ref, wb_ref,
    onehot_ref, slope_ref, slope_total_ref, state_ref, halo_ref, gathered_ref,
    slots_ref,
):
    frames = onehot_ref.shape[0]
    beads = cot_ref.shape[1] // frames
    back = read_halo(bf_ref, bs_ref)
    cot_own = (cot_own_ref[...] + mul_nt(back, select_ref[...])).astype(BF16)
    cot = cot_ref[...] + mul(wa_ref[1], cot_own)
    cot_low = cot.astype(BF16)
    state = state_ref[...]
    grad_b = mul_nt(gathered_ref[...], cot_low)
    cot_gathered = mul(wb_ref[0], cot_low) * 0.5
    grad_c = mul_nt(state, (cot_gathered * slope_total_ref[...]).astype(BF16))
    cot_gathered = cot_gathered.astype(BF16)
    cot_halo, grad_a = None, None
    for frame in range(frames):
        lanes = slice(frame * beads, (frame + 1) * beads)
        part = scatter(onehot_ref, slope_ref, cot_gathered, frame, beads)
        here = mul_nt(state[:, lanes], part[:, :beads].astype(BF16))
        grad_a = here if grad_a is None else grad_a + here
        cot_halo = part[:, beads:] if cot_halo is None else cot_halo + part[:, beads:]
    grad_a = grad_a + mul_nt(halo_ref[...], cot_halo.astype(BF16))
    put_slots(slots_ref, me_ref[0], [grad_a, grad_c, grad_b])


def finish_kernel(me_ref, *refs):
    *sources, wa_ref, wc_ref, wb_ref, readout_ref = refs
    me = me_ref[0]
    count = len(sources) // 2
    rows = (sources[0].shape[0] - TAIL) // 6
    total = jnp.zeros(readout_ref.shape, F32)
    for slot in range(2 * count):
        source = sources[slot ^ (count - 1)]
        chunk = jnp.bitwise_xor(me, slot)
        place = pl.ds(pl.multiple_of(chunk * rows, rows), rows)
        for layer, base in ((0, 0), (1, 3 * rows)):
            for number, ref in enumerate((wa_ref, wc_ref, wb_ref)):
                ref[layer, place, :] = source[base + number * rows : base + (number + 1) * rows, :].astype(F32)
        total = jnp.where(chunk == 0, source[6 * rows :, :].astype(F32)[0], total)
    readout_ref[...] = total


def kernel_call(body, outs, args, scratch=(), flops=0, smem=0, far=0, limit=24):
    spaces = [pltpu.SMEM] * smem + [pltpu.HBM] * far + [pltpu.VMEM] * (len(args) - smem - far)
    args = [pltpu.with_memory_space_constraint(a, pltpu.HBM) if s is pltpu.HBM else a for a, s in zip(args, spaces)]
    return pl.pallas_call(
        body,
        out_shape=outs,
        in_specs=[pl.BlockSpec(memory_space=space) for space in spaces],
        out_specs=jax.tree.map(
            lambda out: pl.BlockSpec(memory_space=pltpu.HBM if getattr(out, "memory_space", None) is pltpu.HBM else pltpu.VMEM), outs
        ),
        scratch_shapes=list(scratch),
        compiler_params=pltpu.CompilerParams(vmem_limit_bytes=limit * MEBI),
        cost_estimate=pl.CostEstimate(flops=flops, bytes_accessed=0, transcendentals=0),
    )(*args)


def near(shape, dtype=BF16):
    return pltpu.VMEM(shape, dtype)


def swapped(value, kind):
    count = lax.axis_size(RING)
    if kind == 0:
        pairs = [(s, s ^ 1) for s in range(count)]
    else:
        pairs = [(s, (s + 1) % count if s % 2 else (s - 1) % count) for s in range(count)]
    return lax.ppermute(value, RING, pairs)


def partner(value, axis, bits):
    return lax.ppermute(value, axis, [(s, s ^ bits) for s in range(lax.axis_size(axis))])


def summed(*terms):
    terms = [term.astype(F32) for term in terms]
    while len(terms) > 1:
        terms = [terms[n] + terms[n + 1] if n + 1 < len(terms) else terms[n] for n in range(0, len(terms), 2)]
    return terms[0].astype(BF16)


def powers(bounds):
    return jnp.clip(jnp.ceil(jnp.log2(jnp.maximum(bounds, 1e-37))), -120.0, 120.0)


def scaled(part):
    count, rows, width = part.shape
    body, readout = part[:, :-TAIL].reshape(count, 6, -1, width), part[:, rows - TAIL : rows - TAIL + 1]
    power = powers(jnp.concatenate([jnp.abs(readout), jnp.max(jnp.abs(body), axis=2)], axis=1))
    factor = jnp.exp2(-power)
    body = (body * factor[:, 1:, None]).reshape(count, -1, width)
    return jnp.concatenate([body, readout * factor[:, :1], power], axis=1).astype(F16)


def restored(sent):
    rows, width = sent.shape
    sent = sent.astype(F32)
    factor = jnp.exp2(sent[rows - TAIL + 1 :])
    body = sent[:-TAIL].reshape(6, -1, width) * factor[1:, None]
    readout = sent[rows - TAIL : rows - TAIL + 1] * factor[:1]
    return jnp.concatenate([body.reshape(-1, width), readout, jnp.zeros((TAIL - 1, width), F32)], axis=0)


def plane(value, x, y):
    rep, dom, tp = (lax.axis_size(a) for a in EVERY)
    flip = (2 * dom * tp if x else 0) + (1 if y else 0)
    return lax.ppermute(value, EVERY, [(s, s ^ flip) for s in range(rep * dom * tp)])


def along_dom(mine):
    count, bit = lax.axis_size("dom"), 1
    while bit < count:
        flips = [bit] if 2 * bit >= count else [3 * bit, 2 * bit, bit]
        mine = summed(mine, *[partner(mine, "dom", flip) for flip in flips])
        bit *= 4
    return mine


def core_sum(slots):
    return slots[:4] + partner(slots[4:], "rep", 1)


def reduce_parts(parts):
    part = jnp.concatenate(parts, axis=1)
    sent = scaled(part[1:])
    terms = [restored(plane(sent[0], 0, 1)), restored(plane(sent[1], 1, 0)), restored(plane(sent[2], 1, 1))]
    mine = along_dom(summed(part[0], *terms))
    return [plane(mine, 1, 1), plane(mine, 1, 0), plane(mine, 0, 1), mine]


def local(features, radial, neighbours, halo_lists, slab_counts, frame_labels, w_a, w_c, w_b, readout):
    frames, beads, channels = features.shape
    hidden, layers = w_a.shape[2], w_a.shape[0]
    degree, halo = radial.shape[1], halo_lists.shape[2]
    lanes, halo_lanes = frames * beads, 2 * frames * halo
    rows = beads + halo_lanes
    scale = (2.0 / (frames * lax.axis_size("rep"))) / math.sqrt(beads * lax.axis_size(RING))
    rep = lax.axis_index("rep")
    me = (lax.rem(rep, 2) * 4 + (rep // 2) * 2 + lax.axis_index("tp")).astype(jnp.int32)
    where = jnp.stack([me, lax.rem(lax.axis_index(RING), 2).astype(jnp.int32)])

    half = (channels // 2, halo_lanes)
    state, select, first, second, neigh, weight = kernel_call(
        select_kernel,
        (
            near((channels, lanes)),
            near((lanes, halo_lanes)),
            near(half),
            near(half),
            near(neighbours.shape, jnp.int32),
            near(radial.shape),
        ),
        (where, features, halo_lists, neighbours, radial),
        scratch=[
            pltpu.VMEM(features.shape, BF16),
            pltpu.VMEM(halo_lists.shape, jnp.int32),
            pltpu.SemaphoreType.DMA((4,)),
        ],
        smem=1,
        far=4,
    )
    second, first = swapped(second, 1), swapped(first, 0)
    weights = [near((layers, channels, hidden)), near((layers, channels, hidden)), near((layers, hidden, channels))]
    turned = near((hidden, channels))
    onehot_type = near((frames, rows, degree * beads))
    onehot, edge, wa, wc, wb, readout_near, wta, wtb, own, cross = kernel_call(
        functools.partial(prepare_kernel, halo),
        (
            onehot_type,
            near((frames, degree, SUB, beads)),
            *weights,
            near(readout.shape, F32),
            turned,
            turned,
            near((hidden, lanes)),
            near((hidden, lanes), F32),
        ),
        (where, w_a, w_c, w_b, readout, state, neigh, weight),
        scratch=[
            pltpu.VMEM(neighbours.shape, jnp.int32),
            pltpu.SemaphoreType.DMA((4,)),
        ],
        smem=1,
        far=4,
        flops=2 * 10**9,
    )
    totals = (hidden, lanes)
    edge_slopes = (frames, hidden, degree * beads)
    state1, first, second, halo0, gathered0, slope0, slope_total0 = kernel_call(
        first_kernel,
        (
            near((channels, lanes)),
            near(half),
            near(half),
            near((channels, halo_lanes)),
            near(totals),
            near(edge_slopes),
            near(totals, F32),
        ),
        (second, first, onehot, edge, wta, wtb, own, cross, state, select),
        scratch=[pltpu.VMEM(totals, F32)],
        flops=4 * 10**9,
    )
    wta, wtb, own, cross, wide, live, sign = kernel_call(
        later_kernel,
        (
            turned, turned, near((hidden, lanes)), near((hidden, lanes), F32), near((channels, beads), F32),
            near((1, lanes), F32), near((1, lanes), F32),
        ),
        (jnp.concatenate([slab_counts[:, 0], frame_labels]), state1, wa, wc, wb, readout_near),
        smem=1,
        flops=10**8,
    )
    second, first = swapped(second, 1), swapped(first, 0)
    energy, grad_readout, cot, first, second, cot_own, cot_halo, cot_cross, halo1, gathered1, cot_low1 = kernel_call(
        functools.partial(middle_kernel, scale),
        (
            jax.ShapeDtypeStruct((frames, beads), F32),
            near((SUB, channels), F32),
            near((channels, lanes), F32),
            near(half),
            near(half),
            near(totals, F32),
            near((hidden, halo_lanes)),
            near(totals),
            near((channels, halo_lanes)),
            near(totals),
            near((channels, lanes)),
        ),
        (second, first, onehot, edge, wta, wtb, wb, own, cross, state1, live, sign, wide),
        scratch=[pltpu.VMEM(edge_slopes, BF16), pltpu.VMEM(totals, F32), pltpu.VMEM(totals, F32)],
        flops=6 * 10**9,
    )
    second, first = swapped(second, 1), swapped(first, 0)
    chunk = hidden // 8
    upper_slots, cot = kernel_call(
        upper_grads_kernel,
        (near((8, 3 * chunk + TAIL, channels), F32), near((channels, lanes), F32)),
        (where, state1, halo1, gathered1, cot_low1, cot_own, cot_halo, cot_cross, grad_readout, cot, wc),
        smem=1,
        flops=10**8,
    )
    lower_slots = kernel_call(
        lower_kernel,
        near((8, 3 * chunk, channels), F32),
        (
            where, first, second, select, cot_own, cot, wa, wb,
            onehot, slope0, slope_total0, state, halo0, gathered0,
        ),
        smem=1,
        flops=4 * 10**9,
    )
    close = reduce_parts([jnp.concatenate([lower_slots[:4], upper_slots[:4]], axis=1) + partner(jnp.concatenate([lower_slots[4:], upper_slots[4:]], axis=1), "rep", 1)])
    far = [partner(value, "rep", 1) for value in close]
    grad = jax.ShapeDtypeStruct((layers, channels, hidden), F32)
    grad_wa, grad_wc, grad_wb, grad_readout = kernel_call(
        finish_kernel,
        (grad, grad, grad, jax.ShapeDtypeStruct((channels,), F32)),
        (where, *close, *far),
        smem=1,
    )
    return grad_wa, grad_wc, grad_wb, grad_readout, energy


def solution(mesh):
    placed = (
        P("rep", RING, None),
        P("rep", None, RING),
        P("rep", None, RING),
        P("rep", None, RING),
        P("rep", RING),
        P("rep"),
        P(),
        P(),
        P(),
        P(),
    )
    return jax.shard_map(
        local,
        mesh=mesh,
        in_specs=placed,
        out_specs=(P(), P(), P(), P(), P("rep", RING)),
        check_vma=False,
    )
```

```python
import functools
import math

import jax
import jax.numpy as jnp
from jax import lax
from jax.experimental import pallas as pl
from jax.experimental.pallas import tpu as pltpu
from jax.sharding import PartitionSpec as P

BF16, F16, F32 = jnp.bfloat16, jnp.float16, jnp.float32
MEBI = 1024 * 1024
SUB = 16
TAIL = 8
RING = ("dom", "tp")
EVERY = ("rep", "dom", "tp")


def mul(a, b):
    return jnp.dot(a, b, preferred_element_type=F32)


def mul_nt(a, b):
    return lax.dot_general(a, b, (((1,), (1,)), ((), ())), preferred_element_type=F32)


def mul_tn(a, b):
    return lax.dot_general(a, b, (((0,), (0,)), ((), ())), preferred_element_type=F32)


def packed_halves(both):
    rows, lanes = both.shape[0] // 2, both.shape[1] // 2
    low, high = both[:rows], both[rows:]
    first = jnp.concatenate([low[:, :lanes], high[:, :lanes]], axis=1)
    second = jnp.concatenate([low[:, lanes:], high[:, lanes:]], axis=1)
    return first, second


def unpacked_halves(first, second):
    lanes = first.shape[1] // 2
    low = jnp.concatenate([first[:, :lanes], second[:, :lanes]], axis=1)
    high = jnp.concatenate([first[:, lanes:], second[:, lanes:]], axis=1)
    return jnp.concatenate([low, high], axis=0)


def send_lanes(even, list_ref, beads):
    parts = []
    for side in range(2):
        for frame in range(list_ref.shape[0]):
            down, up = list_ref[frame, 0:1, :], list_ref[frame, 1:2, :]
            parts.append((jnp.where(even, down, up) if side else jnp.where(even, up, down)) + frame * beads)
    return jnp.concatenate(parts, axis=1)


def write_halo(first_ref, second_ref, both):
    first, second = packed_halves(both)
    first_ref[...] = first.astype(BF16)
    second_ref[...] = second.astype(BF16)


def read_halo(first_ref, second_ref):
    return unpacked_halves(first_ref[...].astype(F32), second_ref[...].astype(F32)).astype(BF16)


def copies_of(pairs, sems):
    copies = [pltpu.make_async_copy(source, target, sems.at[n]) for n, (source, target) in enumerate(pairs)]
    for copy in copies:
        copy.start()
    return copies


def select_kernel(
    where_ref, feat_hbm, list_hbm, neigh_hbm, radial_hbm,
    state_ref, select_ref, first_ref, second_ref, neigh_ref, radial_ref,
    feat_ref, list_ref, sems,
):
    pairs = [(list_hbm, list_ref), (feat_hbm, feat_ref), (neigh_hbm, neigh_ref), (radial_hbm, radial_ref)]
    list_copy, feat_copy, *others = copies_of(pairs, sems)
    list_copy.wait()
    frames, beads, channels = feat_ref.shape
    lanes = frames * beads
    sent = send_lanes(where_ref[1] == 0, list_ref, beads)
    row = lax.broadcasted_iota(jnp.int32, (lanes, sent.shape[1]), 0)
    select = jnp.where(row == sent, 1.0, 0.0).astype(BF16)
    feat_copy.wait()
    state = feat_ref[...].reshape(lanes, channels).astype(F32).T.astype(BF16)
    write_halo(first_ref, second_ref, mul(state, select))
    state_ref[...] = state
    select_ref[...] = select
    for copy in others:
        copy.wait()


def write_onehot(onehot_ref, slots_ref):
    frames, degree, beads = slots_ref.shape
    row = lax.broadcasted_iota(jnp.int32, (onehot_ref.shape[1], beads), 0)
    for frame in range(frames):
        for slot in range(degree):
            hit = row == slots_ref[frame, slot : slot + 1, :]
            onehot_ref[frame, :, slot * beads : (slot + 1) * beads] = jnp.where(hit, 1.0, 0.0).astype(BF16)


def prepare_kernel(
    halo, where_ref, wa_hbm, wc_hbm, wb_hbm, readout_hbm, state_ref, neigh_ref, radial_ref,
    onehot_ref, edge_ref, wa_ref, wc_ref, wb_ref, readout_ref, wta_ref, wtb_ref, own_ref, cross_ref,
    slots_ref, sems,
):
    frames, degree, beads = neigh_ref.shape
    pairs = [(wa_hbm, wa_ref), (wc_hbm, wc_ref), (wb_hbm, wb_ref), (readout_hbm, readout_ref)]
    copies = copies_of(pairs, sems)
    odd = where_ref[1] != 0
    for frame in range(frames):
        neigh = neigh_ref[frame]
        weight = jnp.where(neigh >= 0, radial_ref[frame].astype(F32), 0.0)
        entry = neigh - beads
        upper = entry >= halo
        entry = jnp.where(upper, entry - halo, entry) + (beads + frame * halo)
        upper = jnp.where(upper, 1, 0)
        side = jnp.where(odd, upper, 1 - upper)
        slots_ref[frame] = jnp.where(neigh < beads, neigh, entry + side * (frames * halo))
        for slot in range(degree):
            edge_ref[frame, slot] = jnp.broadcast_to(weight[slot : slot + 1, :], (SUB, beads)).astype(BF16)
    write_onehot(onehot_ref, slots_ref)
    for copy in copies:
        copy.wait()
    turned = wa_ref[0].astype(F32).T.astype(BF16)
    wta_ref[...] = turned
    wtb_ref[...] = wb_ref[0].astype(F32).T.astype(BF16)
    own_ref[...] = mul(turned, state_ref[...]).astype(BF16)
    cross_ref[...] = mul(wc_ref[0].astype(F32).T.astype(BF16), state_ref[...])


def later_kernel(
    frame_ref, state_ref, wa_ref, wc_ref, wb_ref, readout_ref, wta_ref, wtb_ref, own_ref, cross_ref, wide_ref, live_ref, sign_ref
):
    last = wa_ref.shape[0] - 1
    turned_a, turned_c, turned_b = (ref[last].astype(F32).T.astype(BF16) for ref in (wa_ref, wc_ref, wb_ref))
    wta_ref[...] = turned_a
    wtb_ref[...] = turned_b
    own_ref[...] = mul(turned_a, state_ref[...]).astype(BF16)
    cross_ref[...] = mul(turned_c, state_ref[...])
    wide = readout_ref[...].reshape(1, -1)
    beads = wide_ref.shape[1]
    wide_ref[...] = jnp.broadcast_to(wide, (beads, wide.shape[1])).T
    frames = live_ref.shape[1] // beads
    bead = lax.broadcasted_iota(jnp.int32, (1, beads), 1)
    for frame in range(frames):
        live = jnp.where(bead < frame_ref[frame], 1.0, 0.0)
        here = slice(frame * beads, (frame + 1) * beads)
        live_ref[:, here] = live
        sign_ref[:, here] = jnp.where(frame_ref[frames + frame] == 0, live, -live)


def edges(onehot_ref, edge_ref, own, halo, cross, slope_ref, total_ref, slope_total_ref, group=4):
    frames, degree, _, beads = edge_ref.shape
    hidden = own.shape[0]
    blocks = hidden // SUB
    for frame in range(frames):
        lanes = slice(frame * beads, (frame + 1) * beads)
        table = jnp.concatenate([own[:, lanes], halo], axis=1) * jnp.asarray(0.5, BF16)
        half_cross = cross[:, lanes] * 0.5
        wide_cross = jnp.concatenate([half_cross] * group, axis=1)
        total_ref[:, lanes] = jnp.zeros((hidden, beads), F32)
        slope_total_ref[:, lanes] = jnp.zeros((hidden, beads), F32)

        def step(index, carry):
            at = slice(index * group * beads, (index + 1) * group * beads)
            half = (mul(table, onehot_ref[frame, :, at]) + wide_cross).astype(BF16)
            turn = jnp.tanh(half)
            rise = 1 + turn
            rest = 1 + half * (1 - turn)
            act_sum, slope_sum = None, None
            kept = []
            for part in range(group):
                here = slice(part * beads, (part + 1) * beads)
                weight = edge_ref[frame, index * group + part]
                weighted = (rise[:, here].reshape(blocks, SUB, beads) * weight[None]).reshape(hidden, beads)
                a = half[:, here] * weighted
                s = rest[:, here] * weighted
                kept.append(s)
                act_sum = a if act_sum is None else act_sum + a
                slope_sum = s if slope_sum is None else slope_sum + s
            slope_ref[frame, :, at] = jnp.concatenate(kept, axis=1)
            total_ref[:, lanes] += act_sum.astype(F32)
            slope_total_ref[:, lanes] += slope_sum.astype(F32)
            return carry

        for index in range(degree // group):
            step(index, 0)


def scatter(onehot_ref, slope_ref, cot_gathered, frame, beads, group=8):
    count = slope_ref.shape[2] // beads
    lanes = slice(frame * beads, (frame + 1) * beads)
    wide = jnp.concatenate([cot_gathered[:, lanes]] * group, axis=1)
    total = None
    for index in range(count // group):
        at = slice(index * group * beads, (index + 1) * group * beads)
        part = mul_nt(slope_ref[frame, :, at] * wide, onehot_ref[frame, :, at])
        total = part if total is None else total + part
    return total


def first_kernel(
    hs_ref, hf_ref, onehot_ref, edge_ref, wta_ref, wtb_ref, own_ref, cross_ref, state_ref, select_ref,
    next_ref, first_ref, second_ref, halo_ref, gathered_ref, slope_ref, slope_total_ref,
    total_ref,
):
    halo = read_halo(hf_ref, hs_ref)
    halo_ref[...] = halo
    halo_rows = mul(wta_ref[...], halo).astype(BF16)
    edges(onehot_ref, edge_ref, own_ref[...], halo_rows, cross_ref[...], slope_ref, total_ref, slope_total_ref)
    gathered = total_ref[...].astype(BF16)
    gathered_ref[...] = gathered
    state = (state_ref[...].astype(F32) + mul(wtb_ref[...], gathered)).astype(BF16)
    next_ref[...] = state
    write_halo(first_ref, second_ref, mul(state, select_ref[...]))


def middle_kernel(
    scale,
    hs_ref, hf_ref, onehot_ref, edge_ref, wta_ref, wtb_ref, wb_ref, own_ref, cross_ref, state_ref, live_ref, sign_ref, readout_ref,
    energy_ref, grad_readout_ref, cot_ref, first_ref, second_ref, cot_own_ref, cot_halo_ref, cot_cross_ref,
    halo_ref, gathered_ref, cot_low_ref,
    slope_ref, slope_total_ref, total_ref,
):
    last = wb_ref.shape[0] - 1
    beads = edge_ref.shape[3]
    frames = edge_ref.shape[0]
    halo = read_halo(hf_ref, hs_ref)
    halo_ref[...] = halo
    state = state_ref[...]
    halo_rows = mul(wta_ref[...], halo).astype(BF16)
    edges(onehot_ref, edge_ref, own_ref[...], halo_rows, cross_ref[...], slope_ref, total_ref, slope_total_ref)
    gathered = total_ref[...].astype(BF16)
    gathered_ref[...] = gathered
    final = (state.astype(F32) + mul(wtb_ref[...], gathered)).astype(BF16).astype(F32)
    sigmoid = jax.nn.sigmoid(final)
    activated = final * sigmoid
    readout = jnp.concatenate([readout_ref[...]] * frames, axis=1)
    live = live_ref[...]
    sign = sign_ref[...]
    energy = live * jnp.sum(activated * readout, axis=0, keepdims=True)
    for frame in range(frames):
        energy_ref[frame : frame + 1, :] = energy[:, frame * beads : (frame + 1) * beads]
    signs = jnp.broadcast_to(sign, (SUB, sign.shape[1])).astype(BF16)
    grad_readout_ref[...] = mul_nt(signs, activated.astype(BF16)) * scale
    cot = (sign * scale) * readout * (sigmoid * (1.0 + final * (1.0 - sigmoid)))
    cot_ref[...] = cot
    cot_low = cot.astype(BF16)
    cot_low_ref[...] = cot_low
    cot_gathered = mul(wb_ref[last], cot_low) * 0.5
    cot_cross_ref[...] = (cot_gathered * slope_total_ref[...]).astype(BF16)
    cot_gathered = cot_gathered.astype(BF16)
    cot_halo = None
    for frame in range(frames):
        part = scatter(onehot_ref, slope_ref, cot_gathered, frame, beads)
        cot_own_ref[:, frame * beads : (frame + 1) * beads] = part[:, :beads]
        cot_halo = part[:, beads:] if cot_halo is None else cot_halo + part[:, beads:]
    write_halo(first_ref, second_ref, cot_halo)
    cot_halo_ref[...] = cot_halo.astype(BF16)


def put_slots(slots_ref, me, grads):
    slots = slots_ref.shape[0]
    rows = grads[0].shape[0] // slots
    for chunk in range(slots):
        slot = jnp.bitwise_xor(me, chunk)
        for number, grad in enumerate(grads):
            start = number * rows
            slots_ref[slot, start : start + rows, :] = grad[chunk * rows : (chunk + 1) * rows]


def upper_grads_kernel(
    me_ref, state_ref, halo_ref, gathered_ref, cot_low_ref, cot_own_ref, cot_halo_ref, cot_cross_ref, grad_readout_ref,
    cot_ref, wc_ref,
    slots_ref, base_ref,
):
    me = me_ref[0]
    state = state_ref[...]
    grad_a = mul_nt(state, cot_own_ref[...].astype(BF16)) + mul_nt(halo_ref[...], cot_halo_ref[...])
    grad_c = mul_nt(state, cot_cross_ref[...])
    grad_b = mul_nt(gathered_ref[...], cot_low_ref[...])
    row = lax.broadcasted_iota(jnp.int32, (TAIL, slots_ref.shape[2]), 0)
    tail = jnp.where(row == 0, grad_readout_ref[:TAIL], 0.0)
    for slot in range(slots_ref.shape[0]):
        slots_ref[slot, slots_ref.shape[1] - TAIL :, :] = tail
    put_slots(slots_ref, me, [grad_a, grad_c, grad_b])
    base_ref[...] = cot_ref[...] + mul(wc_ref[1], cot_cross_ref[...])


def lower_kernel(
    me_ref, bf_ref, bs_ref, select_ref, cot_own_ref, cot_ref, wa_ref, wb_ref,
    onehot_ref, slope_ref, slope_total_ref, state_ref, halo_ref, gathered_ref,
    slots_ref,
):
    frames = onehot_ref.shape[0]
    beads = cot_ref.shape[1] // frames
    back = read_halo(bf_ref, bs_ref)
    cot_own = (cot_own_ref[...] + mul_nt(back, select_ref[...])).astype(BF16)
    cot = cot_ref[...] + mul(wa_ref[1], cot_own)
    cot_low = cot.astype(BF16)
    state = state_ref[...]
    grad_b = mul_nt(gathered_ref[...], cot_low)
    cot_gathered = mul(wb_ref[0], cot_low) * 0.5
    grad_c = mul_nt(state, (cot_gathered * slope_total_ref[...]).astype(BF16))
    cot_gathered = cot_gathered.astype(BF16)
    cot_halo, grad_a = None, None
    for frame in range(frames):
        lanes = slice(frame * beads, (frame + 1) * beads)
        part = scatter(onehot_ref, slope_ref, cot_gathered, frame, beads)
        here = mul_nt(state[:, lanes], part[:, :beads].astype(BF16))
        grad_a = here if grad_a is None else grad_a + here
        cot_halo = part[:, beads:] if cot_halo is None else cot_halo + part[:, beads:]
    grad_a = grad_a + mul_nt(halo_ref[...], cot_halo.astype(BF16))
    put_slots(slots_ref, me_ref[0], [grad_a, grad_c, grad_b])


def finish_kernel(me_ref, *refs):
    *sources, wa_ref, wc_ref, wb_ref, readout_ref = refs
    me = me_ref[0]
    count = len(sources) // 2
    rows = (sources[0].shape[0] - TAIL) // 6
    total = jnp.zeros(readout_ref.shape, F32)
    for slot in range(2 * count):
        source = sources[slot ^ (count - 1)]
        chunk = jnp.bitwise_xor(me, slot)
        place = pl.ds(pl.multiple_of(chunk * rows, rows), rows)
        for layer, base in ((0, 0), (1, 3 * rows)):
            for number, ref in enumerate((wa_ref, wc_ref, wb_ref)):
                ref[layer, place, :] = source[base + number * rows : base + (number + 1) * rows, :].astype(F32)
        total = jnp.where(chunk == 0, source[6 * rows :, :].astype(F32)[0], total)
    readout_ref[...] = total


def kernel_call(body, outs, args, scratch=(), flops=0, smem=0, far=0, limit=24):
    spaces = [pltpu.SMEM] * smem + [pltpu.HBM] * far + [pltpu.VMEM] * (len(args) - smem - far)
    args = [pltpu.with_memory_space_constraint(a, pltpu.HBM) if s is pltpu.HBM else a for a, s in zip(args, spaces)]
    return pl.pallas_call(
        body,
        out_shape=outs,
        in_specs=[pl.BlockSpec(memory_space=space) for space in spaces],
        out_specs=jax.tree.map(
            lambda out: pl.BlockSpec(memory_space=pltpu.HBM if getattr(out, "memory_space", None) is pltpu.HBM else pltpu.VMEM), outs
        ),
        scratch_shapes=list(scratch),
        compiler_params=pltpu.CompilerParams(vmem_limit_bytes=limit * MEBI),
        cost_estimate=pl.CostEstimate(flops=flops, bytes_accessed=0, transcendentals=0),
    )(*args)


def near(shape, dtype=BF16):
    return pltpu.VMEM(shape, dtype)


def swapped(value, kind):
    count = lax.axis_size(RING)
    if kind == 0:
        pairs = [(s, s ^ 1) for s in range(count)]
    else:
        pairs = [(s, (s + 1) % count if s % 2 else (s - 1) % count) for s in range(count)]
    return lax.ppermute(value, RING, pairs)


def partner(value, axis, bits):
    return lax.ppermute(value, axis, [(s, s ^ bits) for s in range(lax.axis_size(axis))])


def summed(*terms):
    terms = [term.astype(F32) for term in terms]
    while len(terms) > 1:
        terms = [terms[n] + terms[n + 1] if n + 1 < len(terms) else terms[n] for n in range(0, len(terms), 2)]
    return terms[0].astype(BF16)


def powers(bounds):
    return jnp.clip(jnp.ceil(jnp.log2(jnp.maximum(bounds, 1e-37))), -120.0, 120.0)


def scaled(part):
    count, rows, width = part.shape
    body, readout = part[:, :-TAIL].reshape(count, 6, -1, width), part[:, rows - TAIL : rows - TAIL + 1]
    power = powers(jnp.concatenate([jnp.abs(readout), jnp.max(jnp.abs(body), axis=2)], axis=1))
    factor = jnp.exp2(-power)
    body = (body * factor[:, 1:, None]).reshape(count, -1, width)
    return jnp.concatenate([body, readout * factor[:, :1], power], axis=1).astype(F16)


def restored(sent):
    rows, width = sent.shape
    sent = sent.astype(F32)
    factor = jnp.exp2(sent[rows - TAIL + 1 :])
    body = sent[:-TAIL].reshape(6, -1, width) * factor[1:, None]
    readout = sent[rows - TAIL : rows - TAIL + 1] * factor[:1]
    return jnp.concatenate([body.reshape(-1, width), readout, jnp.zeros((TAIL - 1, width), F32)], axis=0)


def plane(value, x, y):
    rep, dom, tp = (lax.axis_size(a) for a in EVERY)
    flip = (2 * dom * tp if x else 0) + (1 if y else 0)
    return lax.ppermute(value, EVERY, [(s, s ^ flip) for s in range(rep * dom * tp)])


def along_dom(mine):
    count, bit = lax.axis_size("dom"), 1
    while bit < count:
        flips = [bit] if 2 * bit >= count else [2 * bit, 3 * bit, bit]
        mine = summed(mine, *[partner(mine, "dom", flip) for flip in flips])
        bit *= 4
    return mine


def core_sum(slots):
    return slots[:4] + partner(slots[4:], "rep", 1)


def reduce_parts(parts):
    part = jnp.concatenate(parts, axis=1)
    sent = scaled(part[1:])
    terms = [restored(plane(sent[0], 0, 1)), restored(plane(sent[1], 1, 0)), restored(plane(sent[2], 1, 1))]
    mine = along_dom(summed(part[0], *terms))
    return [plane(mine, 1, 1), plane(mine, 1, 0), plane(mine, 0, 1), mine]


def local(features, radial, neighbours, halo_lists, slab_counts, frame_labels, w_a, w_c, w_b, readout):
    frames, beads, channels = features.shape
    hidden, layers = w_a.shape[2], w_a.shape[0]
    degree, halo = radial.shape[1], halo_lists.shape[2]
    lanes, halo_lanes = frames * beads, 2 * frames * halo
    rows = beads + halo_lanes
    scale = (2.0 / (frames * lax.axis_size("rep"))) / math.sqrt(beads * lax.axis_size(RING))
    rep = lax.axis_index("rep")
    me = (lax.rem(rep, 2) * 4 + (rep // 2) * 2 + lax.axis_index("tp")).astype(jnp.int32)
    where = jnp.stack([me, lax.rem(lax.axis_index(RING), 2).astype(jnp.int32)])

    half = (channels // 2, halo_lanes)
    state, select, first, second, neigh, weight = kernel_call(
        select_kernel,
        (
            near((channels, lanes)),
            near((lanes, halo_lanes)),
            near(half),
            near(half),
            near(neighbours.shape, jnp.int32),
            near(radial.shape),
        ),
        (where, features, halo_lists, neighbours, radial),
        scratch=[
            pltpu.VMEM(features.shape, BF16),
            pltpu.VMEM(halo_lists.shape, jnp.int32),
            pltpu.SemaphoreType.DMA((4,)),
        ],
        smem=1,
        far=4,
    )
    second, first = swapped(second, 1), swapped(first, 0)
    weights = [near((layers, channels, hidden)), near((layers, channels, hidden)), near((layers, hidden, channels))]
    turned = near((hidden, channels))
    onehot_type = near((frames, rows, degree * beads))
    onehot, edge, wa, wc, wb, readout_near, wta, wtb, own, cross = kernel_call(
        functools.partial(prepare_kernel, halo),
        (
            onehot_type,
            near((frames, degree, SUB, beads)),
            *weights,
            near(readout.shape, F32),
            turned,
            turned,
            near((hidden, lanes)),
            near((hidden, lanes), F32),
        ),
        (where, w_a, w_c, w_b, readout, state, neigh, weight),
        scratch=[
            pltpu.VMEM(neighbours.shape, jnp.int32),
            pltpu.SemaphoreType.DMA((4,)),
        ],
        smem=1,
        far=4,
        flops=2 * 10**9,
    )
    totals = (hidden, lanes)
    edge_slopes = (frames, hidden, degree * beads)
    state1, first, second, halo0, gathered0, slope0, slope_total0 = kernel_call(
        first_kernel,
        (
            near((channels, lanes)),
            near(half),
            near(half),
            near((channels, halo_lanes)),
            near(totals),
            near(edge_slopes),
            near(totals, F32),
        ),
        (second, first, onehot, edge, wta, wtb, own, cross, state, select),
        scratch=[pltpu.VMEM(totals, F32)],
        flops=4 * 10**9,
    )
    wta, wtb, own, cross, wide, live, sign = kernel_call(
        later_kernel,
        (
            turned, turned, near((hidden, lanes)), near((hidden, lanes), F32), near((channels, beads), F32),
            near((1, lanes), F32), near((1, lanes), F32),
        ),
        (jnp.concatenate([slab_counts[:, 0], frame_labels]), state1, wa, wc, wb, readout_near),
        smem=1,
        flops=10**8,
    )
    second, first = swapped(second, 1), swapped(first, 0)
    energy, grad_readout, cot, first, second, cot_own, cot_halo, cot_cross, halo1, gathered1, cot_low1 = kernel_call(
        functools.partial(middle_kernel, scale),
        (
            jax.ShapeDtypeStruct((frames, beads), F32),
            near((SUB, channels), F32),
            near((channels, lanes), F32),
            near(half),
            near(half),
            near(totals, F32),
            near((hidden, halo_lanes)),
            near(totals),
            near((channels, halo_lanes)),
            near(totals),
            near((channels, lanes)),
        ),
        (second, first, onehot, edge, wta, wtb, wb, own, cross, state1, live, sign, wide),
        scratch=[pltpu.VMEM(edge_slopes, BF16), pltpu.VMEM(totals, F32), pltpu.VMEM(totals, F32)],
        flops=6 * 10**9,
    )
    second, first = swapped(second, 1), swapped(first, 0)
    chunk = hidden // 8
    upper_slots, cot = kernel_call(
        upper_grads_kernel,
        (near((8, 3 * chunk + TAIL, channels), F32), near((channels, lanes), F32)),
        (where, state1, halo1, gathered1, cot_low1, cot_own, cot_halo, cot_cross, grad_readout, cot, wc),
        smem=1,
        flops=10**8,
    )
    lower_slots = kernel_call(
        lower_kernel,
        near((8, 3 * chunk, channels), F32),
        (
            where, first, second, select, cot_own, cot, wa, wb,
            onehot, slope0, slope_total0, state, halo0, gathered0,
        ),
        smem=1,
        flops=4 * 10**9,
    )
    close = reduce_parts([jnp.concatenate([lower_slots[:4], upper_slots[:4]], axis=1) + partner(jnp.concatenate([lower_slots[4:], upper_slots[4:]], axis=1), "rep", 1)])
    far = [partner(value, "rep", 1) for value in close]
    grad = jax.ShapeDtypeStruct((layers, channels, hidden), F32)
    grad_wa, grad_wc, grad_wb, grad_readout = kernel_call(
        finish_kernel,
        (grad, grad, grad, jax.ShapeDtypeStruct((channels,), F32)),
        (where, *close, *far),
        smem=1,
    )
    return grad_wa, grad_wc, grad_wb, grad_readout, energy


def solution(mesh):
    placed = (
        P("rep", RING, None),
        P("rep", None, RING),
        P("rep", None, RING),
        P("rep", None, RING),
        P("rep", RING),
        P("rep"),
        P(),
        P(),
        P(),
        P(),
    )
    return jax.shard_map(
        local,
        mesh=mesh,
        in_specs=placed,
        out_specs=(P(), P(), P(), P(), P("rep", RING)),
        check_vma=False,
    )
```

```python
import functools
import math

import jax
import jax.numpy as jnp
from jax import lax
from jax.experimental import pallas as pl
from jax.experimental.pallas import tpu as pltpu
from jax.sharding import PartitionSpec as P

BF16, F16, F32 = jnp.bfloat16, jnp.float16, jnp.float32
MEBI = 1024 * 1024
SUB = 16
TAIL = 8
RING = ("dom", "tp")
EVERY = ("rep", "dom", "tp")


def mul(a, b):
    return jnp.dot(a, b, preferred_element_type=F32)


def mul_nt(a, b):
    return lax.dot_general(a, b, (((1,), (1,)), ((), ())), preferred_element_type=F32)


def mul_tn(a, b):
    return lax.dot_general(a, b, (((0,), (0,)), ((), ())), preferred_element_type=F32)


def packed_halves(both):
    rows, lanes = both.shape[0] // 2, both.shape[1] // 2
    low, high = both[:rows], both[rows:]
    first = jnp.concatenate([low[:, :lanes], high[:, :lanes]], axis=1)
    second = jnp.concatenate([low[:, lanes:], high[:, lanes:]], axis=1)
    return first, second


def unpacked_halves(first, second):
    lanes = first.shape[1] // 2
    low = jnp.concatenate([first[:, :lanes], second[:, :lanes]], axis=1)
    high = jnp.concatenate([first[:, lanes:], second[:, lanes:]], axis=1)
    return jnp.concatenate([low, high], axis=0)


def send_lanes(even, list_ref, beads):
    parts = []
    for side in range(2):
        for frame in range(list_ref.shape[0]):
            down, up = list_ref[frame, 0:1, :], list_ref[frame, 1:2, :]
            parts.append((jnp.where(even, down, up) if side else jnp.where(even, up, down)) + frame * beads)
    return jnp.concatenate(parts, axis=1)


def write_halo(first_ref, second_ref, both):
    first, second = packed_halves(both)
    first_ref[...] = first.astype(BF16)
    second_ref[...] = second.astype(BF16)


def read_halo(first_ref, second_ref):
    return unpacked_halves(first_ref[...].astype(F32), second_ref[...].astype(F32)).astype(BF16)


def copies_of(pairs, sems):
    copies = [pltpu.make_async_copy(source, target, sems.at[n]) for n, (source, target) in enumerate(pairs)]
    for copy in copies:
        copy.start()
    return copies


def select_kernel(
    where_ref, feat_hbm, list_hbm, neigh_hbm, radial_hbm,
    state_ref, select_ref, first_ref, second_ref, neigh_ref, radial_ref,
    feat_ref, list_ref, sems,
):
    pairs = [(list_hbm, list_ref), (feat_hbm, feat_ref), (neigh_hbm, neigh_ref), (radial_hbm, radial_ref)]
    list_copy, feat_copy, *others = copies_of(pairs, sems)
    list_copy.wait()
    frames, beads, channels = feat_ref.shape
    lanes = frames * beads
    sent = send_lanes(where_ref[1] == 0, list_ref, beads)
    row = lax.broadcasted_iota(jnp.int32, (lanes, sent.shape[1]), 0)
    select = jnp.where(row == sent, 1.0, 0.0).astype(BF16)
    feat_copy.wait()
    state = feat_ref[...].reshape(lanes, channels).astype(F32).T.astype(BF16)
    write_halo(first_ref, second_ref, mul(state, select))
    state_ref[...] = state
    select_ref[...] = select
    for copy in others:
        copy.wait()


def write_onehot(onehot_ref, slots_ref):
    frames, degree, beads = slots_ref.shape
    row = lax.broadcasted_iota(jnp.int32, (onehot_ref.shape[1], beads), 0)
    for frame in range(frames):
        for slot in range(degree):
            hit = row == slots_ref[frame, slot : slot + 1, :]
            onehot_ref[frame, :, slot * beads : (slot + 1) * beads] = jnp.where(hit, 1.0, 0.0).astype(BF16)


def prepare_kernel(
    halo, where_ref, wa_hbm, wc_hbm, wb_hbm, readout_hbm, state_ref, neigh_ref, radial_ref,
    onehot_ref, edge_ref, wa_ref, wc_ref, wb_ref, readout_ref, wta_ref, wtb_ref, own_ref, cross_ref,
    slots_ref, sems,
):
    frames, degree, beads = neigh_ref.shape
    pairs = [(wa_hbm, wa_ref), (wc_hbm, wc_ref), (wb_hbm, wb_ref), (readout_hbm, readout_ref)]
    copies = copies_of(pairs, sems)
    odd = where_ref[1] != 0
    for frame in range(frames):
        neigh = neigh_ref[frame]
        weight = jnp.where(neigh >= 0, radial_ref[frame].astype(F32), 0.0)
        entry = neigh - beads
        upper = entry >= halo
        entry = jnp.where(upper, entry - halo, entry) + (beads + frame * halo)
        upper = jnp.where(upper, 1, 0)
        side = jnp.where(odd, upper, 1 - upper)
        slots_ref[frame] = jnp.where(neigh < beads, neigh, entry + side * (frames * halo))
        for slot in range(degree):
            edge_ref[frame, slot] = jnp.broadcast_to(weight[slot : slot + 1, :], (SUB, beads)).astype(BF16)
    write_onehot(onehot_ref, slots_ref)
    for copy in copies:
        copy.wait()
    turned = wa_ref[0].astype(F32).T.astype(BF16)
    wta_ref[...] = turned
    wtb_ref[...] = wb_ref[0].astype(F32).T.astype(BF16)
    own_ref[...] = mul(turned, state_ref[...]).astype(BF16)
    cross_ref[...] = mul(wc_ref[0].astype(F32).T.astype(BF16), state_ref[...])


def later_kernel(
    frame_ref, state_ref, wa_ref, wc_ref, wb_ref, readout_ref, wta_ref, wtb_ref, own_ref, cross_ref, wide_ref, live_ref, sign_ref
):
    last = wa_ref.shape[0] - 1
    turned_a, turned_c, turned_b = (ref[last].astype(F32).T.astype(BF16) for ref in (wa_ref, wc_ref, wb_ref))
    wta_ref[...] = turned_a
    wtb_ref[...] = turned_b
    own_ref[...] = mul(turned_a, state_ref[...]).astype(BF16)
    cross_ref[...] = mul(turned_c, state_ref[...])
    wide = readout_ref[...].reshape(1, -1)
    beads = wide_ref.shape[1]
    wide_ref[...] = jnp.broadcast_to(wide, (beads, wide.shape[1])).T
    frames = live_ref.shape[1] // beads
    bead = lax.broadcasted_iota(jnp.int32, (1, beads), 1)
    for frame in range(frames):
        live = jnp.where(bead < frame_ref[frame], 1.0, 0.0)
        here = slice(frame * beads, (frame + 1) * beads)
        live_ref[:, here] = live
        sign_ref[:, here] = jnp.where(frame_ref[frames + frame] == 0, live, -live)


def edges(onehot_ref, edge_ref, own, halo, cross, slope_ref, total_ref, slope_total_ref, group=4):
    frames, degree, _, beads = edge_ref.shape
    hidden = own.shape[0]
    blocks = hidden // SUB
    for frame in range(frames):
        lanes = slice(frame * beads, (frame + 1) * beads)
        table = jnp.concatenate([own[:, lanes], halo], axis=1) * jnp.asarray(0.5, BF16)
        half_cross = cross[:, lanes] * 0.5
        wide_cross = jnp.concatenate([half_cross] * group, axis=1)
        total_ref[:, lanes] = jnp.zeros((hidden, beads), F32)
        slope_total_ref[:, lanes] = jnp.zeros((hidden, beads), F32)

        def step(index, carry):
            at = slice(index * group * beads, (index + 1) * group * beads)
            half = (mul(table, onehot_ref[frame, :, at]) + wide_cross).astype(BF16)
            turn = jnp.tanh(half)
            rise = 1 + turn
            rest = 1 + half * (1 - turn)
            act_sum, slope_sum = None, None
            kept = []
            for part in range(group):
                here = slice(part * beads, (part + 1) * beads)
                weight = edge_ref[frame, index * group + part]
                weighted = (rise[:, here].reshape(blocks, SUB, beads) * weight[None]).reshape(hidden, beads)
                a = half[:, here] * weighted
                s = rest[:, here] * weighted
                kept.append(s)
                act_sum = a if act_sum is None else act_sum + a
                slope_sum = s if slope_sum is None else slope_sum + s
            slope_ref[frame, :, at] = jnp.concatenate(kept, axis=1)
            total_ref[:, lanes] += act_sum.astype(F32)
            slope_total_ref[:, lanes] += slope_sum.astype(F32)
            return carry

        for index in range(degree // group):
            step(index, 0)


def scatter(onehot_ref, slope_ref, cot_gathered, frame, beads, group=8):
    count = slope_ref.shape[2] // beads
    lanes = slice(frame * beads, (frame + 1) * beads)
    wide = jnp.concatenate([cot_gathered[:, lanes]] * group, axis=1)
    total = None
    for index in range(count // group):
        at = slice(index * group * beads, (index + 1) * group * beads)
        part = mul_nt(slope_ref[frame, :, at] * wide, onehot_ref[frame, :, at])
        total = part if total is None else total + part
    return total


def first_kernel(
    hs_ref, hf_ref, onehot_ref, edge_ref, wta_ref, wtb_ref, own_ref, cross_ref, state_ref, select_ref,
    next_ref, first_ref, second_ref, halo_ref, gathered_ref, slope_ref, slope_total_ref,
    total_ref,
):
    halo = read_halo(hf_ref, hs_ref)
    halo_ref[...] = halo
    halo_rows = mul(wta_ref[...], halo).astype(BF16)
    edges(onehot_ref, edge_ref, own_ref[...], halo_rows, cross_ref[...], slope_ref, total_ref, slope_total_ref)
    gathered = total_ref[...].astype(BF16)
    gathered_ref[...] = gathered
    state = (state_ref[...].astype(F32) + mul(wtb_ref[...], gathered)).astype(BF16)
    next_ref[...] = state
    write_halo(first_ref, second_ref, mul(state, select_ref[...]))


def middle_kernel(
    scale,
    hs_ref, hf_ref, onehot_ref, edge_ref, wta_ref, wtb_ref, wb_ref, own_ref, cross_ref, state_ref, live_ref, sign_ref, readout_ref,
    energy_ref, grad_readout_ref, cot_ref, first_ref, second_ref, cot_own_ref, cot_halo_ref, cot_cross_ref,
    halo_ref, gathered_ref, cot_low_ref,
    slope_ref, slope_total_ref, total_ref,
):
    last = wb_ref.shape[0] - 1
    beads = edge_ref.shape[3]
    frames = edge_ref.shape[0]
    halo = read_halo(hf_ref, hs_ref)
    halo_ref[...] = halo
    state = state_ref[...]
    halo_rows = mul(wta_ref[...], halo).astype(BF16)
    edges(onehot_ref, edge_ref, own_ref[...], halo_rows, cross_ref[...], slope_ref, total_ref, slope_total_ref)
    gathered = total_ref[...].astype(BF16)
    gathered_ref[...] = gathered
    final = (state.astype(F32) + mul(wtb_ref[...], gathered)).astype(BF16).astype(F32)
    sigmoid = jax.nn.sigmoid(final)
    activated = final * sigmoid
    readout = jnp.concatenate([readout_ref[...]] * frames, axis=1)
    live = live_ref[...]
    sign = sign_ref[...]
    energy = live * jnp.sum(activated * readout, axis=0, keepdims=True)
    for frame in range(frames):
        energy_ref[frame : frame + 1, :] = energy[:, frame * beads : (frame + 1) * beads]
    signs = jnp.broadcast_to(sign, (SUB, sign.shape[1])).astype(BF16)
    grad_readout_ref[...] = mul_nt(signs, activated.astype(BF16)) * scale
    cot = (sign * scale) * readout * (sigmoid * (1.0 + final * (1.0 - sigmoid)))
    cot_ref[...] = cot
    cot_low = cot.astype(BF16)
    cot_low_ref[...] = cot_low
    cot_gathered = mul(wb_ref[last], cot_low) * 0.5
    cot_cross_ref[...] = (cot_gathered * slope_total_ref[...]).astype(BF16)
    cot_gathered = cot_gathered.astype(BF16)
    cot_halo = None
    for frame in range(frames):
        part = scatter(onehot_ref, slope_ref, cot_gathered, frame, beads)
        cot_own_ref[:, frame * beads : (frame + 1) * beads] = part[:, :beads]
        cot_halo = part[:, beads:] if cot_halo is None else cot_halo + part[:, beads:]
    write_halo(first_ref, second_ref, cot_halo)
    cot_halo_ref[...] = cot_halo.astype(BF16)


def put_slots(slots_ref, me, grads):
    slots = slots_ref.shape[0]
    rows = grads[0].shape[0] // slots
    for chunk in range(slots):
        slot = jnp.bitwise_xor(me, chunk)
        for number, grad in enumerate(grads):
            start = number * rows
            slots_ref[slot, start : start + rows, :] = grad[chunk * rows : (chunk + 1) * rows]


def upper_grads_kernel(
    me_ref, state_ref, halo_ref, gathered_ref, cot_low_ref, cot_own_ref, cot_halo_ref, cot_cross_ref, grad_readout_ref,
    cot_ref, wc_ref,
    slots_ref, base_ref,
):
    me = me_ref[0]
    state = state_ref[...]
    grad_a = mul_nt(state, cot_own_ref[...].astype(BF16)) + mul_nt(halo_ref[...], cot_halo_ref[...])
    grad_c = mul_nt(state, cot_cross_ref[...])
    grad_b = mul_nt(gathered_ref[...], cot_low_ref[...])
    row = lax.broadcasted_iota(jnp.int32, (TAIL, slots_ref.shape[2]), 0)
    tail = jnp.where(row == 0, grad_readout_ref[:TAIL], 0.0)
    for slot in range(slots_ref.shape[0]):
        slots_ref[slot, slots_ref.shape[1] - TAIL :, :] = tail
    put_slots(slots_ref, me, [grad_a, grad_c, grad_b])
    base_ref[...] = cot_ref[...] + mul(wc_ref[1], cot_cross_ref[...])


def lower_kernel(
    me_ref, bf_ref, bs_ref, select_ref, cot_own_ref, cot_ref, wa_ref, wb_ref,
    onehot_ref, slope_ref, slope_total_ref, state_ref, halo_ref, gathered_ref,
    slots_ref,
):
    frames = onehot_ref.shape[0]
    beads = cot_ref.shape[1] // frames
    back = read_halo(bf_ref, bs_ref)
    cot_own = (cot_own_ref[...] + mul_nt(back, select_ref[...])).astype(BF16)
    cot = cot_ref[...] + mul(wa_ref[1], cot_own)
    cot_low = cot.astype(BF16)
    state = state_ref[...]
    grad_b = mul_nt(gathered_ref[...], cot_low)
    cot_gathered = mul(wb_ref[0], cot_low) * 0.5
    grad_c = mul_nt(state, (cot_gathered * slope_total_ref[...]).astype(BF16))
    cot_gathered = cot_gathered.astype(BF16)
    cot_halo, grad_a = None, None
    for frame in range(frames):
        lanes = slice(frame * beads, (frame + 1) * beads)
        part = scatter(onehot_ref, slope_ref, cot_gathered, frame, beads)
        here = mul_nt(state[:, lanes], part[:, :beads].astype(BF16))
        grad_a = here if grad_a is None else grad_a + here
        cot_halo = part[:, beads:] if cot_halo is None else cot_halo + part[:, beads:]
    grad_a = grad_a + mul_nt(halo_ref[...], cot_halo.astype(BF16))
    put_slots(slots_ref, me_ref[0], [grad_a, grad_c, grad_b])


def finish_kernel(me_ref, *refs):
    *sources, wa_ref, wc_ref, wb_ref, readout_ref = refs
    me = me_ref[0]
    count = len(sources) // 2
    rows = (sources[0].shape[0] - TAIL) // 6
    total = jnp.zeros(readout_ref.shape, F32)
    for slot in range(2 * count):
        source = sources[slot ^ (count - 1)]
        chunk = jnp.bitwise_xor(me, slot)
        place = pl.ds(pl.multiple_of(chunk * rows, rows), rows)
        for layer, base in ((0, 0), (1, 3 * rows)):
            for number, ref in enumerate((wa_ref, wc_ref, wb_ref)):
                ref[layer, place, :] = source[base + number * rows : base + (number + 1) * rows, :].astype(F32)
        total = jnp.where(chunk == 0, source[6 * rows :, :].astype(F32)[0], total)
    readout_ref[...] = total


def kernel_call(body, outs, args, scratch=(), flops=0, smem=0, far=0, limit=24):
    spaces = [pltpu.SMEM] * smem + [pltpu.HBM] * far + [pltpu.VMEM] * (len(args) - smem - far)
    args = [pltpu.with_memory_space_constraint(a, pltpu.HBM) if s is pltpu.HBM else a for a, s in zip(args, spaces)]
    return pl.pallas_call(
        body,
        out_shape=outs,
        in_specs=[pl.BlockSpec(memory_space=space) for space in spaces],
        out_specs=jax.tree.map(
            lambda out: pl.BlockSpec(memory_space=pltpu.HBM if getattr(out, "memory_space", None) is pltpu.HBM else pltpu.VMEM), outs
        ),
        scratch_shapes=list(scratch),
        compiler_params=pltpu.CompilerParams(vmem_limit_bytes=limit * MEBI),
        cost_estimate=pl.CostEstimate(flops=flops, bytes_accessed=0, transcendentals=0),
    )(*args)


def near(shape, dtype=BF16):
    return pltpu.VMEM(shape, dtype)


def swapped(value, kind):
    count = lax.axis_size(RING)
    if kind == 0:
        pairs = [(s, s ^ 1) for s in range(count)]
    else:
        pairs = [(s, (s + 1) % count if s % 2 else (s - 1) % count) for s in range(count)]
    return lax.ppermute(value, RING, pairs)


def partner(value, axis, bits):
    return lax.ppermute(value, axis, [(s, s ^ bits) for s in range(lax.axis_size(axis))])


def summed(*terms):
    terms = [term.astype(F32) for term in terms]
    while len(terms) > 1:
        terms = [terms[n] + terms[n + 1] if n + 1 < len(terms) else terms[n] for n in range(0, len(terms), 2)]
    return terms[0].astype(BF16)


def powers(bounds):
    return jnp.clip(jnp.ceil(jnp.log2(jnp.maximum(bounds, 1e-37))), -120.0, 120.0)


def scaled(part):
    count, rows, width = part.shape
    body, readout = part[:, :-TAIL].reshape(count, 6, -1, width), part[:, rows - TAIL : rows - TAIL + 1]
    power = powers(jnp.concatenate([jnp.abs(readout), jnp.max(jnp.abs(body), axis=2)], axis=1))
    factor = jnp.exp2(-power)
    body = (body * factor[:, 1:, None]).reshape(count, -1, width)
    return jnp.concatenate([body, readout * factor[:, :1], power], axis=1).astype(F16)


def restored(sent):
    rows, width = sent.shape
    sent = sent.astype(F32)
    factor = jnp.exp2(sent[rows - TAIL + 1 :])
    body = sent[:-TAIL].reshape(6, -1, width) * factor[1:, None]
    readout = sent[rows - TAIL : rows - TAIL + 1] * factor[:1]
    return jnp.concatenate([body.reshape(-1, width), readout, jnp.zeros((TAIL - 1, width), F32)], axis=0)


def plane(value, x, y):
    rep, dom, tp = (lax.axis_size(a) for a in EVERY)
    flip = (2 * dom * tp if x else 0) + (1 if y else 0)
    return lax.ppermute(value, EVERY, [(s, s ^ flip) for s in range(rep * dom * tp)])


def along_dom(mine):
    count, bit = lax.axis_size("dom"), 1
    while bit < count:
        flips = [bit] if 2 * bit >= count else [2 * bit, 3 * bit, bit]
        mine = summed(mine, *[partner(mine, "dom", flip) for flip in flips])
        bit *= 4
    return mine


def core_sum(slots):
    return slots[:4] + partner(slots[4:], "rep", 1)


def reduce_parts(parts):
    part = jnp.concatenate(parts, axis=1)
    sent = scaled(part[1:])
    terms = [restored(plane(sent[1], 1, 0)), restored(plane(sent[2], 1, 1)), restored(plane(sent[0], 0, 1))]
    mine = along_dom(summed(part[0], *terms))
    return [plane(mine, 1, 1), plane(mine, 1, 0), plane(mine, 0, 1), mine]


def local(features, radial, neighbours, halo_lists, slab_counts, frame_labels, w_a, w_c, w_b, readout):
    frames, beads, channels = features.shape
    hidden, layers = w_a.shape[2], w_a.shape[0]
    degree, halo = radial.shape[1], halo_lists.shape[2]
    lanes, halo_lanes = frames * beads, 2 * frames * halo
    rows = beads + halo_lanes
    scale = (2.0 / (frames * lax.axis_size("rep"))) / math.sqrt(beads * lax.axis_size(RING))
    rep = lax.axis_index("rep")
    me = (lax.rem(rep, 2) * 4 + (rep // 2) * 2 + lax.axis_index("tp")).astype(jnp.int32)
    where = jnp.stack([me, lax.rem(lax.axis_index(RING), 2).astype(jnp.int32)])

    half = (channels // 2, halo_lanes)
    state, select, first, second, neigh, weight = kernel_call(
        select_kernel,
        (
            near((channels, lanes)),
            near((lanes, halo_lanes)),
            near(half),
            near(half),
            near(neighbours.shape, jnp.int32),
            near(radial.shape),
        ),
        (where, features, halo_lists, neighbours, radial),
        scratch=[
            pltpu.VMEM(features.shape, BF16),
            pltpu.VMEM(halo_lists.shape, jnp.int32),
            pltpu.SemaphoreType.DMA((4,)),
        ],
        smem=1,
        far=4,
    )
    second, first = swapped(second, 1), swapped(first, 0)
    weights = [near((layers, channels, hidden)), near((layers, channels, hidden)), near((layers, hidden, channels))]
    turned = near((hidden, channels))
    onehot_type = near((frames, rows, degree * beads))
    onehot, edge, wa, wc, wb, readout_near, wta, wtb, own, cross = kernel_call(
        functools.partial(prepare_kernel, halo),
        (
            onehot_type,
            near((frames, degree, SUB, beads)),
            *weights,
            near(readout.shape, F32),
            turned,
            turned,
            near((hidden, lanes)),
            near((hidden, lanes), F32),
        ),
        (where, w_a, w_c, w_b, readout, state, neigh, weight),
        scratch=[
            pltpu.VMEM(neighbours.shape, jnp.int32),
            pltpu.SemaphoreType.DMA((4,)),
        ],
        smem=1,
        far=4,
        flops=2 * 10**9,
    )
    totals = (hidden, lanes)
    edge_slopes = (frames, hidden, degree * beads)
    state1, first, second, halo0, gathered0, slope0, slope_total0 = kernel_call(
        first_kernel,
        (
            near((channels, lanes)),
            near(half),
            near(half),
            near((channels, halo_lanes)),
            near(totals),
            near(edge_slopes),
            near(totals, F32),
        ),
        (second, first, onehot, edge, wta, wtb, own, cross, state, select),
        scratch=[pltpu.VMEM(totals, F32)],
        flops=4 * 10**9,
    )
    wta, wtb, own, cross, wide, live, sign = kernel_call(
        later_kernel,
        (
            turned, turned, near((hidden, lanes)), near((hidden, lanes), F32), near((channels, beads), F32),
            near((1, lanes), F32), near((1, lanes), F32),
        ),
        (jnp.concatenate([slab_counts[:, 0], frame_labels]), state1, wa, wc, wb, readout_near),
        smem=1,
        flops=10**8,
    )
    second, first = swapped(second, 1), swapped(first, 0)
    energy, grad_readout, cot, first, second, cot_own, cot_halo, cot_cross, halo1, gathered1, cot_low1 = kernel_call(
        functools.partial(middle_kernel, scale),
        (
            jax.ShapeDtypeStruct((frames, beads), F32),
            near((SUB, channels), F32),
            near((channels, lanes), F32),
            near(half),
            near(half),
            near(totals, F32),
            near((hidden, halo_lanes)),
            near(totals),
            near((channels, halo_lanes)),
            near(totals),
            near((channels, lanes)),
        ),
        (second, first, onehot, edge, wta, wtb, wb, own, cross, state1, live, sign, wide),
        scratch=[pltpu.VMEM(edge_slopes, BF16), pltpu.VMEM(totals, F32), pltpu.VMEM(totals, F32)],
        flops=6 * 10**9,
    )
    second, first = swapped(second, 1), swapped(first, 0)
    chunk = hidden // 8
    upper_slots, cot = kernel_call(
        upper_grads_kernel,
        (near((8, 3 * chunk + TAIL, channels), F32), near((channels, lanes), F32)),
        (where, state1, halo1, gathered1, cot_low1, cot_own, cot_halo, cot_cross, grad_readout, cot, wc),
        smem=1,
        flops=10**8,
    )
    lower_slots = kernel_call(
        lower_kernel,
        near((8, 3 * chunk, channels), F32),
        (
            where, first, second, select, cot_own, cot, wa, wb,
            onehot, slope0, slope_total0, state, halo0, gathered0,
        ),
        smem=1,
        flops=4 * 10**9,
    )
    close = reduce_parts([jnp.concatenate([lower_slots[:4], upper_slots[:4]], axis=1) + partner(jnp.concatenate([lower_slots[4:], upper_slots[4:]], axis=1), "rep", 1)])
    far = [partner(value, "rep", 1) for value in close]
    grad = jax.ShapeDtypeStruct((layers, channels, hidden), F32)
    grad_wa, grad_wc, grad_wb, grad_readout = kernel_call(
        finish_kernel,
        (grad, grad, grad, jax.ShapeDtypeStruct((channels,), F32)),
        (where, *close, *far),
        smem=1,
    )
    return grad_wa, grad_wc, grad_wb, grad_readout, energy


def solution(mesh):
    placed = (
        P("rep", RING, None),
        P("rep", None, RING),
        P("rep", None, RING),
        P("rep", None, RING),
        P("rep", RING),
        P("rep"),
        P(),
        P(),
        P(),
        P(),
    )
    return jax.shard_map(
        local,
        mesh=mesh,
        in_specs=placed,
        out_specs=(P(), P(), P(), P(), P("rep", RING)),
        check_vma=False,
    )
```
